32 devices in a mesh: chain: 8 (over y, x, core), sector: 4 (over z).
Axes of the slice: x: 2, y: 2, z: 4, core: 2. Of those that a mesh axis runs over, the one named last changes fastest.
Arguments:
- psi: float32 [8, 16, 256, 256], P('chain', 'sector'), may hold values from -6 to 6
- kept_rank: int32 [8, 16], P('chain', 'sector'), may hold values from 64 to 256, as said below
- step_size: float32 [8, 3], P('chain'), may hold values from 0.2 to 0.6
- left_env: bfloat16 [8, 2, 16, 256, 256], P('chain', None, 'sector'), may hold values from -0.375 to 0.375
- right_env: bfloat16 [8, 2, 16, 256, 256], P('chain', None, 'sector'), may hold values from -0.375 to 0.375
- hop_left: bfloat16 [8, 2, 16, 256, 256], P('chain', None, 'sector'), may hold values from -0.375 to 0.375
- hop_right: bfloat16 [8, 2, 16, 256, 256], P('chain', None, 'sector'), may hold values from -0.375 to 0.375
- hop_source: int32 [2, 16], replicated, may hold values from 0 to 15, each once within a row
Outputs:
- site_state: float32 [8, 16, 256, 256], P('chain', 'sector')
- merged_left: float32 [8, 2, 16, 256, 256], P('chain', None, 'sector')
- merged_right: float32 [8, 2, 16, 256, 256], P('chain', None, 'sector')
The draws below stay inside these ranges and needn't reach their ends.
Inputs may be any that keep to these rules, and one draw needn't show every extreme that they name: `kept_rank`: each partition has one sector whose kept rank is the full 256.
All inputs are finite; a program needn't handle non-finite values.
Results may differ from the reference program's by a relative error of at most 0.009.
Values may be sent and summed in bfloat16 or wider, within the bound.
No kernel may reach another device: no remote copies, remote signals or barrier semaphores. Data moves between devices by JAX's collectives and lax.ppermute only.
A program may use at most 64 MiB of HBM per device.

```python
import jax
import jax.numpy as jnp
from jax import lax

BLK = 256
TERMS = 2
HOPS = 2
STEPS = 3
SECT = 16
CHI = 4096
PARTS_SIZE = 8


def draw_kept_rank(key, part):
    first_key = jax.random.fold_in(key, 11)
    second_key = jax.random.fold_in(key, 23)
    ranks = jax.random.randint(first_key, (PARTS_SIZE, SECT), BLK // 4, BLK + 1)
    chosen = jax.random.randint(second_key, (PARTS_SIZE,), 0, SECT)
    column = lax.broadcasted_iota(jnp.int32, (PARTS_SIZE, SECT), 1)
    return jnp.where(column == chosen[:, None], BLK, ranks).astype(jnp.int32)


def block_levels(rng, shape, cuts, low, largest):
    gain = 1.0
    for axis_at, shards_of in cuts:
        steps = jax.random.uniform(jax.random.fold_in(jax.random.fold_in(rng, 6), axis_at), (shards_of,), jnp.float32, low / len(cuts), largest / len(cuts))
        gain = gain * jnp.repeat(jnp.exp(steps), shape[axis_at] // shards_of).reshape((-1,) + (1,) * (len(shape) - 1 - axis_at))
    return gain


def centred(rng, dims, scale, bound, split=(), held_as=jnp.bfloat16):
    factor_of = block_levels(rng, dims, split, -0.22, 0.18) if split else 1.0
    result = jax.random.normal(rng, dims, jnp.float32) * scale * factor_of
    return jnp.minimum(jnp.maximum(result, -bound), bound).astype(held_as)


def setup_inputs(seed: int = 0) -> dict:
    key_list = jax.random.split(jax.random.key(seed), 9)
    return {
        "psi": centred(key_list[0], (PARTS_SIZE, SECT, BLK, BLK), 1.0, 6.0, ((0, 8), (1, 4)), jnp.float32),
        "kept_rank": draw_kept_rank(jax.random.fold_in(key_list[8], 71), 0),
        "step_size": jnp.clip(0.2 + 0.400000021 * jax.random.uniform(key_list[2], (PARTS_SIZE, STEPS), jnp.float32) ** block_levels(key_list[2], (PARTS_SIZE, STEPS), ((0, 8),), -0.2, 0.2), 0.2, 0.6),
        "left_env": centred(key_list[3], (PARTS_SIZE, TERMS, SECT, BLK, BLK), BLK ** -0.5, 0.375, ((0, 8), (2, 4))),
        "right_env": centred(key_list[4], (PARTS_SIZE, TERMS, SECT, BLK, BLK), BLK ** -0.5, 0.375, ((0, 8), (2, 4))),
        "hop_left": centred(key_list[5], (PARTS_SIZE, HOPS, SECT, BLK, BLK), BLK ** -0.5, 0.375, ((0, 8), (2, 4))),
        "hop_right": centred(key_list[6], (PARTS_SIZE, HOPS, SECT, BLK, BLK), BLK ** -0.5, 0.375, ((0, 8), (2, 4))),
        "hop_source": jax.vmap(lambda own: jax.random.permutation(own, SECT))(jax.random.split(key_list[7], HOPS)).reshape((HOPS, SECT)).astype(jnp.int32),
    }


def apply_operator(state, left_env, right_env, hop_left, hop_right, hop_source, mask):
    f32 = jnp.float32
    state_b = state.astype(jnp.bfloat16)
    inner = jnp.einsum('atij,tjk->atik', left_env.astype(f32), state_b.astype(f32)).astype(jnp.bfloat16)
    image = jnp.einsum('atik,atkl->til', inner.astype(f32), right_env.astype(f32))
    picked = state_b[hop_source]
    hop_inner = jnp.einsum('btij,btjk->btik', hop_left.astype(f32), picked.astype(f32)).astype(jnp.bfloat16)
    image = image + jnp.einsum('btik,btkl->til', hop_inner.astype(f32), hop_right.astype(f32))
    return image * mask

def reference(psi, kept_rank, step_size, left_env, right_env, hop_left, hop_right, hop_source):
    f32 = jnp.float32

    def one_part(items):
        block, ranks, steps, left_one, right_one, hop_a, hop_b = items
        row_index = lax.broadcasted_iota(jnp.int32, (SECT, BLK), 1)
        kept_rows = (row_index < ranks[:, None]).astype(f32)
        mask = kept_rows[:, :, None] * kept_rows[:, None, :]
        state = block * mask
        for step in range(STEPS):
            image = apply_operator(state, left_one, right_one, hop_a, hop_b, hop_source, mask)
            self_dot = jnp.sum(state * state)
            cross = jnp.sum(state * image)
            quotient = cross / self_dot
            state = state - steps[step] * (image - quotient * state)
            state = state / jnp.sqrt(jnp.sum(state * state))
        final_b = state.astype(jnp.bfloat16).astype(f32)
        left_half = jnp.einsum('tji,atjk->atik', final_b, left_one.astype(f32)).astype(jnp.bfloat16)
        left_new = CHI * jnp.einsum('atik,tkl->atil', left_half.astype(f32), final_b)
        right_half = jnp.einsum('atij,tkj->atik', right_one.astype(f32), final_b).astype(jnp.bfloat16)
        right_new = CHI * jnp.einsum('tij,atjk->atik', final_b, right_half.astype(f32))
        return (state, left_new, right_new)
    site_state, left_new, right_new = lax.map(one_part, (psi, kept_rank, step_size, left_env, right_env, hop_left, hop_right))
    zeros_one = jnp.zeros((1, TERMS, SECT, BLK, BLK), f32)
    merged_left = left_env.astype(f32) + jnp.concatenate([zeros_one, left_new[:-1]], axis=0)
    merged_right = right_env.astype(f32) + jnp.concatenate([right_new[1:], zeros_one], axis=0)
    return (site_state, merged_left, merged_right)
```

```python
import functools

import jax
import jax.numpy as jnp
from jax import lax
from jax.experimental import pallas as pl
from jax.experimental.pallas import tpu as pltpu
from jax.sharding import PartitionSpec as P

STEPS = 3
LANES = 128
F32 = jnp.float32
BF16 = jnp.bfloat16


def from_behind(value, axis, steps):
    count = lax.axis_size(axis)
    initial, last = (max(0, -steps), min(count, count - steps))
    return lax.ppermute(value, axis, [(source, source + steps) for source in range(initial, last)])


def dot(a, b):
    return jnp.dot(a, b, preferred_element_type=F32)


def mask_of(rank, size):
    rows = lax.broadcasted_iota(jnp.int32, (size, size), 0)
    cols = lax.broadcasted_iota(jnp.int32, (size, size), 1)
    return (rows < rank) & (cols < rank)


def weights(sums_ref, step_now):
    total = jnp.sum(sums_ref[...], axis=1, keepdims=True)
    self_dot, cross, image_dot = total[0:1], total[1:2], total[2:3]
    quotient = cross / self_dot
    state_resid = cross - quotient * self_dot
    resid_dot = image_dot - 2.0 * quotient * cross + quotient * quotient * self_dot
    new_dot = self_dot - 2.0 * step_now * state_resid + step_now * step_now * resid_dot
    norm = jnp.sqrt(new_dot)
    return (1.0 + step_now * quotient) / norm, -step_now / norm


def lane_sums(value):
    rows = jnp.sum(value, axis=0, keepdims=True)
    total = rows[:, 0:LANES]
    for at in range(LANES, rows.shape[1], LANES):
        total = total + rows[:, at : at + LANES]
    return total


def two_sided(left_ref, right_ref, blocks):
    total = None
    for term, block in enumerate(blocks):
        half = dot(left_ref[term, 0], block).astype(BF16)
        now = dot(half, right_ref[term, 0])
        total = now if total is None else total + now
    return total


def start_kernel(rank_ref, psi_ref, state_ref, block_ref):
    size = psi_ref.shape[-1]
    state = jnp.where(mask_of(rank_ref[pl.program_id(0)], size), psi_ref[0], 0.0)
    state_ref[0] = state
    block_ref[0] = state.astype(BF16)


def site_first_kernel(rank_ref, block_ref, left_ref, right_ref, out_ref):
    terms = left_ref.shape[0]
    out_ref[0] = two_sided(left_ref, right_ref, [block_ref[0]] * terms)


def site_kernel(step, rank_ref, step_ref, sums_ref, state_ref, image_ref, block_ref, left_ref, right_ref, state_out, out_ref):
    size = block_ref.shape[-1]
    terms = left_ref.shape[0]
    keep, turn = weights(sums_ref, step_ref[0, step])
    mask = mask_of(rank_ref[pl.program_id(0)], size)
    site = two_sided(left_ref, right_ref, [block_ref[0]] * terms)
    image = image_ref[0]
    state_out[0] = keep * state_ref[0] + turn * image
    out_ref[0] = keep * image + turn * jnp.where(mask, site, 0.0)


def hop_kernel(step, hops, rank_ref, source_ref, step_ref, *refs):
    picked = refs[:hops]
    left_ref, right_ref, state_ref, base_ref = refs[hops : hops + 4]
    refs = refs[hops + 4 :]
    at = pl.program_id(0)
    size = base_ref.shape[-1]
    mask = mask_of(rank_ref[at], size)
    hop = two_sided(left_ref, right_ref, [ref[0] for ref in picked])
    if step == 0:
        image_ref, block_ref, sums_out = refs
        image = jnp.where(mask, base_ref[0] + hop, 0.0)
    else:
        sums_ref, image_ref, block_ref, sums_out = refs
        _, turn = weights(sums_ref, step_ref[0, step - 1])
        image = base_ref[0] + turn * jnp.where(mask, hop, 0.0)
    image_ref[0] = image
    block_ref[0] = image.astype(BF16)
    state = state_ref[0]

    @pl.when(at == 0)
    def _():
        sums_out[...] = jnp.zeros_like(sums_out)

    sums_out[0:1] += lane_sums(state * state)
    sums_out[1:2] += lane_sums(state * image)
    sums_out[2:3] += lane_sums(image * image)


def last_kernel(step, step_ref, sums_ref, state_ref, image_ref, state_out, block_ref):
    keep, turn = weights(sums_ref, step_ref[0, step])
    state = keep * state_ref[0] + turn * image_ref[0]
    state_out[0] = state
    block_ref[0] = state.astype(BF16)


def merge_kernel(scale, from_left, from_right, left_next, right_next, left_own, right_own, left_out, right_out):
    contract_rows = (((0,), (0,)), ((), ()))
    contract_cols = (((1,), (1,)), ((), ()))
    a = from_left[0]
    b = from_right[0]
    for term in range(left_next.shape[0]):
        half = lax.dot_general(a, left_next[term, 0], contract_rows, preferred_element_type=F32).astype(BF16)
        left_out[term, 0] = left_own[term, 0].astype(F32) + scale * dot(half, a)
        half = lax.dot_general(right_next[term, 0], b, contract_cols, preferred_element_type=F32).astype(BF16)
        right_out[term, 0] = right_own[term, 0].astype(F32) + scale * dot(b, half)


def on_device(psi, kept_rank, step_size, left_env, right_env, hop_left, hop_right, hop_source):
    count, size = psi.shape[1], psi.shape[2]
    terms, hops = left_env.shape[1], hop_left.shape[1]
    chi_total = count * lax.axis_size("sector") * size
    first_sector = lax.axis_index("sector") * count
    sources = lax.dynamic_slice_in_dim(hop_source, first_sector, count, 1)
    rank = kept_rank[0]
    left_one, right_one = left_env[0], right_env[0]
    hop_first, hop_second = hop_left[0], hop_right[0]

    square = pl.BlockSpec((1, size, size), lambda t, *_: (t, 0, 0))
    pair = pl.BlockSpec((terms, 1, size, size), lambda t, *_: (0, t, 0, 0))
    hop_pair = pl.BlockSpec((hops, 1, size, size), lambda t, *_: (0, t, 0, 0))
    sums_spec = pl.BlockSpec((8, LANES), lambda t, *_: (0, 0))
    scalars = pl.BlockSpec(memory_space=pltpu.SMEM)
    block_f32 = jax.ShapeDtypeStruct((count, size, size), F32)
    block_b16 = jax.ShapeDtypeStruct((count, size, size), BF16)
    sums_shape = jax.ShapeDtypeStruct((8, LANES), F32)
    flop = 2 * size**3

    def call(body, prefetch, in_specs, out_specs, out_shape, flops, args):
        moved = sum(a.size * a.dtype.itemsize for a in args[prefetch:])
        moved += sum(s.size * s.dtype.itemsize for s in out_shape)
        return pl.pallas_call(
            body,
            grid_spec=pltpu.PrefetchScalarGridSpec(
                num_scalar_prefetch=prefetch, grid=(count,), in_specs=in_specs, out_specs=out_specs
            ),
            out_shape=out_shape,
            compiler_params=pltpu.CompilerParams(
                dimension_semantics=("arbitrary",), vmem_limit_bytes=32 * 1024 * 1024
            ),
            cost_estimate=pl.CostEstimate(flops=flops, bytes_accessed=moved, transcendentals=0),
        )(*args)

    state, block = call(
        start_kernel, 1, [square], [square, square], [block_f32, block_b16], 0, (rank, psi[0])
    )
    left_next = right_next = None
    sums = image = base = None
    for step in range(STEPS):
        gathered = lax.all_gather(block, "sector", axis=0, tiled=True)
        if step == 0:
            left_next = from_behind(left_one, "chain", 1)
            right_next = from_behind(right_one, "chain", -1)
            (base,) = call(
                site_first_kernel, 1, [square, pair, pair], [square], [block_f32],
                count * terms * 2 * flop, (rank, block, left_one, right_one),
            )
        else:
            state, base = call(
                functools.partial(site_kernel, step - 1), 2,
                [sums_spec, square, square, square, pair, pair], [square, square], [block_f32, block_f32],
                count * terms * 2 * flop,
                (rank, step_size, sums, state, image, block, left_one, right_one),
            )
        picked = [
            pl.BlockSpec((1, size, size), functools.partial(lambda hop, t, rank, src, *_: (src[hop, t], 0, 0), hop))
            for hop in range(hops)
        ]
        extra = [] if step == 0 else [sums]
        image, block, sums = call(
            functools.partial(hop_kernel, step, hops), 3,
            picked + [hop_pair, hop_pair, square, square] + [sums_spec] * len(extra),
            [square, square, sums_spec], [block_f32, block_b16, sums_shape],
            count * hops * 2 * flop,
            (rank, sources, step_size, *([gathered] * hops), hop_first, hop_second, state, base, *extra),
        )
        sums = lax.psum(sums, "sector")
    state, block = call(
        functools.partial(last_kernel, STEPS - 1), 1, [sums_spec, square, square], [square, square],
        [block_f32, block_b16], 0, (step_size, sums, state, image),
    )
    from_left = from_behind(block, "chain", 1)
    from_right = from_behind(block, "chain", -1)
    env_f32 = jax.ShapeDtypeStruct((terms, count, size, size), F32)
    merged_left, merged_right = call(
        functools.partial(merge_kernel, float(chi_total)), 0, [square, square, pair, pair, pair, pair],
        [pair, pair], [env_f32, env_f32], count * terms * 4 * flop,
        (from_left, from_right, left_next, right_next, left_one, right_one),
    )
    return (state[None], merged_left[None], merged_right[None])


def solution(mesh):
    placed = (
        P("chain", "sector", None, None),
        P("chain", "sector"),
        P("chain", None),
        P("chain", None, "sector", None, None),
        P("chain", None, "sector", None, None),
        P("chain", None, "sector", None, None),
        P("chain", None, "sector", None, None),
        P(),
    )
    return jax.shard_map(
        on_device,
        mesh=mesh,
        in_specs=placed,
        out_specs=(
            P("chain", "sector", None, None),
            P("chain", None, "sector", None, None),
            P("chain", None, "sector", None, None),
        ),
        check_vma=False,
    )
```

```python
import functools

import jax
import jax.numpy as jnp
from jax import lax
from jax.experimental import pallas as pl
from jax.experimental.pallas import tpu as pltpu
from jax.sharding import PartitionSpec as P

STEPS = 3
LANES = 128
ROWS = 16
FAR = 1 << 20
F32 = jnp.float32
BF16 = jnp.bfloat16
I32 = jnp.int32
VMEM_BYTES = 56 * 1024 * 1024
PLANS = (
    (16, 11, 16),
    (17, 14, 17),
    (14, 18, 14),
    (22, 11, 22),
    (19, 16, 19),
    (19, 19, 19),
    (24, 17, 24),
    (17, 25, 17),
    (27, 22, 27),
    (32, 32, 32),
)


def from_behind(value, axis, steps):
    count = lax.axis_size(axis)
    initial, last = (max(0, -steps), min(count, count - steps))
    return lax.ppermute(value, axis, [(source, source + steps) for source in range(initial, last)])


def cyclic(value, axis, shift):
    count = lax.axis_size(axis)
    return lax.ppermute(value, axis, [(source, (source + shift) % count) for source in range(count)])


def dot(a, b):
    return jnp.dot(a, b, preferred_element_type=F32)


def mask_of(rank, size):
    rows = lax.broadcasted_iota(I32, (size, size), 0)
    cols = lax.broadcasted_iota(I32, (size, size), 1)
    return (rows < rank) & (cols < rank)


def weights(sums, step_now):
    total = jnp.sum(sums, axis=1, keepdims=True)
    self_dot, cross, image_dot = total[0:1], total[1:2], total[2:3]
    quotient = cross / self_dot
    state_resid = cross - quotient * self_dot
    resid_dot = image_dot - 2.0 * quotient * cross + quotient * quotient * self_dot
    new_dot = self_dot - 2.0 * step_now * state_resid + step_now * step_now * resid_dot
    norm = jnp.sqrt(new_dot)
    return (1.0 + step_now * quotient) / norm, -step_now / norm


def lane_sums(value):
    rows = jnp.sum(value, axis=0, keepdims=True)
    total = rows[:, 0:LANES]
    for at in range(LANES, rows.shape[1], LANES):
        total = total + rows[:, at : at + LANES]
    return total


def head_of(rows, room_ref):
    room_ref[...] = jnp.zeros_like(room_ref)
    for place, row in enumerate(rows):
        for part in range(3):
            now = row.astype(BF16).astype(F32)
            room_ref[3 * part + place : 3 * part + place + 1] = now
            row = row - now
    return room_ref[...].astype(BF16)


def rows_of_head(head, room_ref):
    room_ref[...] = head.astype(F32)
    return room_ref[0:3] + room_ref[3:6] + room_ref[6:9]


def kept_rows(rank):
    return (rank + (ROWS - 1)) & ~(ROWS - 1)


def packed_rows(rank, half):
    rows = kept_rows(rank)
    return jnp.where(rows <= half, rows, 3 * rows - 2 * half)


def at_rows(ref, start, rows):
    return ref.at[pl.ds(pl.multiple_of(start, ROWS), rows), :]


def quarters(value):
    half = value.shape[0] // 2
    return (
        value[:half, :half].astype(BF16),
        value[:half, half:].T.astype(BF16),
        value[half:, :half].astype(BF16),
        value[half:, half:].astype(BF16),
    )


def put_packed(ref, start, rank, parts):
    half = parts[0].shape[0]
    over = jnp.maximum(kept_rows(rank) - half, 0)
    for place, part in zip((0, half, half + over, half + 2 * over), parts):
        at_rows(ref, start + place, half)[...] = part


def get_packed(ref, start, rank, half):
    kept = kept_rows(rank)
    over = jnp.maximum(kept - half, 0)
    row = lax.broadcasted_iota(I32, (half, half), 0)

    def part(place, rows):
        value = at_rows(ref, start + place, half)[...].astype(F32)
        return jnp.where(row < rows, value, 0.0)

    first = part(0, kept).astype(BF16)
    second = part(half, over).T.astype(BF16)
    third = part(half + over, over).astype(BF16)
    fourth = part(half + 2 * over, over).astype(BF16)
    top = jnp.concatenate([first, second], axis=1)
    low = jnp.concatenate([third, fourth], axis=1)
    return jnp.concatenate([top, low], axis=0)


class Layout:
    def __init__(self, ways, count, hops):
        self.ways, self.count, self.hops = ways, count, hops
        self.plan = 0
        self.rank = 1
        self.send = self.rank + count
        self.shift = self.send + (ways - 1) * count
        self.start = self.shift + hops * count
        self.source_rank = self.start + hops * count
        self.size = self.source_rank + hops * count


def plan_kernel(lay, half, plans, me_ref, source_ref, *refs):
    ways, count, hops = lay.ways, lay.count, lay.hops
    rank_refs, (table_ref, need_ref, place_ref, all_ref) = refs[:ways], refs[ways:]
    me = me_ref[0]
    for at in range(ways * count * ways):
        need_ref[at] = 0
    for shift in range(ways):
        owner = lax.rem(me + (ways - shift), ways)
        for at in range(count):
            all_ref[owner * count + at] = rank_refs[shift][at]
    for hop in range(hops):
        for taker in range(ways):
            for at in range(count):
                need_ref[source_ref[hop, taker * count + at] * ways + taker] = 1
    largest = [jnp.int32(0)] * ways
    for owner in range(ways):
        for taker in range(ways):
            if owner == taker:
                continue
            shift = (taker - owner) % ways
            used = jnp.int32(ROWS)
            for at in range(count):
                source = owner * count + at
                needed = need_ref[source * ways + taker] == 1
                rows = packed_rows(all_ref[source], half)

                @pl.when(owner == me)
                def _():
                    table_ref[lay.send + (shift - 1) * count + at] = jnp.where(needed, used, FAR)

                @pl.when(taker == me)
                def _():
                    place_ref[source] = used

                used = used + jnp.where(needed, rows, 0)
            largest[shift] = jnp.maximum(largest[shift], used)
    chosen = jnp.int32(len(plans) - 1)
    for index in reversed(range(len(plans) - 1)):
        fits = largest[1] <= plans[index][0]
        for shift in range(2, ways):
            fits = fits & (largest[shift] <= plans[index][shift - 1])
        chosen = jnp.where(fits, index, chosen)
    table_ref[lay.plan] = chosen
    for at in range(count):
        table_ref[lay.rank + at] = rank_refs[0][at]
        for hop in range(hops):
            source = source_ref[hop, me * count + at]
            owner = lax.div(source, count)
            here = owner == me
            slot = hop * count + at
            table_ref[lay.shift + slot] = lax.rem(me + (ways - owner), ways)
            table_ref[lay.start + slot] = jnp.where(here, (source - owner * count) * (4 * half), place_ref[source])
            table_ref[lay.source_rank + slot] = all_ref[source]


def fill_sends(lay, half, caps, table_ref, at, own_buf, send_bufs):
    packed = at_rows(own_buf, at * 4 * half, 4 * half)[...]
    for shift in range(1, lay.ways):
        start = jnp.minimum(table_ref[lay.send + (shift - 1) * lay.count + at], caps[shift - 1])
        at_rows(send_bufs[shift - 1], start, 4 * half)[...] = packed


def send_copies(send_bufs, send_outs, sems):
    return [
        pltpu.make_async_copy(buf.at[pl.ds(0, out.shape[0]), :], out, sems.at[at])
        for at, (buf, out) in enumerate(zip(send_bufs, send_outs))
    ]


def prepare_kernel(half, rank_ref, psi_ref, state_ref, own_ref):
    rank = rank_ref[pl.program_id(0)]
    value = jnp.where(mask_of(rank, 2 * half), psi_ref[0], 0.0)
    state_ref[0] = value
    put_packed(own_ref, 0, rank, quarters(value))


def send_kernel(lay, half, caps, table_ref, own_ref, *refs):
    number = lay.ways - 1
    send_outs, send_bufs, sems = refs[:number], refs[number : 2 * number], refs[2 * number]
    for buf in send_bufs:
        buf[0:ROWS] = jnp.zeros((ROWS, half), BF16)

    @pl.loop(0, lay.count)
    def _(at):
        fill_sends(lay, half, caps, table_ref, at, own_ref, send_bufs)

    copies = send_copies(send_bufs, send_outs, sems)
    for copy in copies:
        copy.start()
    for copy in copies:
        copy.wait()


def two_sided(left_ref, right_ref, blocks):
    total = None
    for term, block in enumerate(blocks):
        part = dot(left_ref[term, 0], block).astype(BF16)
        now = dot(part, right_ref[term, 0])
        total = now if total is None else total + now
    return total


def site_kernel(lay, half, table_ref, own_ref, left_ref, right_ref, out_ref):
    block = get_packed(own_ref, 0, table_ref[lay.rank + pl.program_id(0)], half)
    out_ref[0] = two_sided(left_ref, right_ref, [block] * left_ref.shape[0])


def hop_kernel(lay, half, caps, table_ref, turn_ref, step_ref, sums_ref, *refs):
    ways, count, hops = lay.ways, lay.count, lay.hops
    size = 2 * half
    refs = list(refs)

    def take(number):
        out = refs[:number]
        del refs[:number]
        return out

    own_in, *packed_in = take(ways)
    left_in, right_in, site_in, state_in, image_in = take(5)
    state_out, image_out, sums_out = take(3)
    own_out, *send_outs = take(ways)
    pool, left, right, site, state, image, room, sems, out_sems = take(9)
    own_buf, *send_bufs = take(ways)

    places = [0, own_in.shape[0]]
    for cap in caps:
        places.append(places[-1] + cap)
    arrivals = [
        pltpu.make_async_copy(ref, pool.at[pl.ds(place, ref.shape[0]), :], sems.at[0, at])
        for at, (ref, place) in enumerate(zip([own_in, *packed_in], places))
    ]

    def inputs(at):
        return [
            pltpu.make_async_copy(left_in.at[:, at], left.at[:, at], sems.at[1, at]),
            pltpu.make_async_copy(right_in.at[:, at], right.at[:, at], sems.at[2, at]),
            pltpu.make_async_copy(site_in.at[at], site.at[at], sems.at[3, at]),
            pltpu.make_async_copy(state_in.at[at], state.at[at], sems.at[4, at]),
            pltpu.make_async_copy(image_in.at[at], image.at[at], sems.at[5, at]),
        ]

    def outputs(at):
        rows = pl.ds(pl.multiple_of(at * 4 * half, ROWS), 4 * half)
        return [
            pltpu.make_async_copy(state.at[at], state_out.at[at], out_sems.at[0, at]),
            pltpu.make_async_copy(image.at[at], image_out.at[at], out_sems.at[1, at]),
            pltpu.make_async_copy(own_buf.at[rows, :], own_out.at[rows, :], out_sems.at[2, at]),
        ]

    for copy in arrivals:
        copy.start()
    for at in range(count):
        for copy in inputs(at):
            copy.start()
    for copy in arrivals:
        copy.wait()

    sums = sums_ref[0:3]
    for place in places[1:ways]:
        sums = sums + rows_of_head(pool[place : place + ROWS], room)
    first = turn_ref[0] == 0
    keep, turn = weights(sums, step_ref[0, jnp.maximum(turn_ref[0] - 1, 0)])
    keep_state = jnp.where(first, 1.0, keep)
    keep_image = jnp.where(first, 0.0, keep)
    turn_state = jnp.where(first, 0.0, turn)
    turn_image = jnp.where(first, 1.0, turn)

    def sector(at, sums):
        for copy in inputs(at):
            copy.wait()
        total = site[at]
        for hop in range(hops):
            slot = hop * count + at
            shift = table_ref[lay.shift + slot]
            start = table_ref[lay.start + slot]
            for way in range(1, ways):
                start = start + jnp.where(shift == way, places[way], 0)
            block = get_packed(pool, start, table_ref[lay.source_rank + slot], half)
            part = dot(left[hop, at], block).astype(BF16)
            total = total + dot(part, right[hop, at])
        rank = table_ref[lay.rank + at]
        before = image[at]
        now = keep_state * state[at] + turn_state * before
        value = keep_image * before + turn_image * jnp.where(mask_of(rank, size), total, 0.0)
        state[at] = now
        image[at] = value
        put_packed(own_buf, at * 4 * half, rank, quarters(value))
        for copy in outputs(at):
            copy.start()
        fill_sends(lay, half, caps, table_ref, at, own_buf, send_bufs)
        return tuple(
            whole + lane_sums(part) for whole, part in zip(sums, (now * now, now * value, value * value))
        )

    rows = lax.fori_loop(0, count, sector, (jnp.zeros((1, LANES), F32),) * 3)
    head = head_of(rows, room)
    for buf in send_bufs:
        buf[0:ROWS] = head
    leaving = send_copies(send_bufs, send_outs, sems.at[0])
    for copy in leaving:
        copy.start()
    sums_out[...] = jnp.zeros_like(sums_out)
    for place, row in enumerate(rows):
        sums_out[place : place + 1] = row
    for copy in leaving:
        copy.wait()
    for at in range(count):
        for copy in outputs(at):
            copy.wait()


def last_kernel(step, step_ref, sums_ref, state_ref, image_ref, state_out, block_ref):
    keep, turn = weights(sums_ref[...], step_ref[0, step])
    state = keep * state_ref[0] + turn * image_ref[0]
    state_out[0] = state
    block_ref[0] = state.astype(BF16)


def merge_kernel(scale, from_left, from_right, left_next, right_next, left_own, right_own, left_out, right_out):
    contract_rows = (((0,), (0,)), ((), ()))
    contract_cols = (((1,), (1,)), ((), ()))
    a = from_left[0]
    b = from_right[0]
    for term in range(left_next.shape[0]):
        part = lax.dot_general(a, left_next[term, 0], contract_rows, preferred_element_type=F32).astype(BF16)
        left_out[term, 0] = left_own[term, 0].astype(F32) + scale * dot(part, a)
        part = lax.dot_general(right_next[term, 0], b, contract_cols, preferred_element_type=F32).astype(BF16)
        right_out[term, 0] = right_own[term, 0].astype(F32) + scale * dot(b, part)


def run_kernel(body, args, in_specs, out_shape, out_specs, *, flops=0, grid=(), scratch=(), reuse=None):
    moved = sum(a.size * a.dtype.itemsize for a in args)
    moved += sum(s.size * s.dtype.itemsize for s in out_shape)
    return pl.pallas_call(
        body,
        grid=grid,
        in_specs=in_specs,
        out_specs=out_specs,
        out_shape=out_shape,
        scratch_shapes=list(scratch),
        input_output_aliases=reuse or {},
        compiler_params=pltpu.CompilerParams(vmem_limit_bytes=VMEM_BYTES),
        cost_estimate=pl.CostEstimate(flops=flops, bytes_accessed=moved, transcendentals=0),
    )(*args)


def on_device(psi, kept_rank, step_size, left_env, right_env, hop_left, hop_right, hop_source):
    count, size = psi.shape[1], psi.shape[2]
    half = size // 2
    terms, hops = left_env.shape[1], hop_left.shape[1]
    ways = lax.axis_size("sector")
    chi_total = count * ways * size
    lay = Layout(ways, count, hops)
    left_one, right_one = left_env[0], right_env[0]
    hop_first, hop_second = hop_left[0], hop_right[0]
    full = count * 4 * half
    plans = [tuple(ROWS * (full * part // (32 * ROWS)) + (ROWS if part == 32 else 0) for part in plan) for plan in PLANS if len(plan) == ways - 1]
    if not plans:
        plans = [(full + ROWS,) * (ways - 1)]

    smem = pl.BlockSpec(memory_space=pltpu.SMEM)
    vmem = pl.BlockSpec(memory_space=pltpu.VMEM)
    anywhere = pl.BlockSpec(memory_space=pl.ANY)
    square = pl.BlockSpec((1, size, size), lambda t: (t, 0, 0))
    packed = pl.BlockSpec((4 * half, half), lambda t: (t, 0))
    pair = pl.BlockSpec((terms, 1, size, size), lambda t: (0, t, 0, 0))
    sums_spec = pl.BlockSpec((8, LANES), lambda t: (0, 0))
    block_f32 = jax.ShapeDtypeStruct((count, size, size), F32)
    block_b16 = jax.ShapeDtypeStruct((count, size, size), BF16)
    own_shape = jax.ShapeDtypeStruct((full, half), BF16)
    sums_shape = jax.ShapeDtypeStruct((8, LANES), F32)
    flop = 2 * size**3

    rank = kept_rank[0]
    ranks = [rank] + [cyclic(rank, "sector", shift) for shift in range(1, ways)]
    left_next = from_behind(left_one, "chain", 1)
    right_next = from_behind(right_one, "chain", -1)
    state, own = run_kernel(
        functools.partial(prepare_kernel, half),
        (rank, psi[0]),
        [smem, square],
        [block_f32, own_shape],
        [square, packed],
        grid=(count,),
    )
    me = lax.axis_index("sector").astype(I32).reshape(1)
    (table,) = run_kernel(
        functools.partial(plan_kernel, lay, half, plans),
        (me, hop_source, *ranks),
        [smem] * (2 + ways),
        [jax.ShapeDtypeStruct((lay.size,), I32)],
        [smem],
        scratch=[
            pltpu.SMEM((ways * count * ways,), I32),
            pltpu.SMEM((ways * count,), I32),
            pltpu.SMEM((ways * count,), I32),
        ],
    )

    def update(caps, state, own, table, step_size, left_one, right_one, hop_first, hop_second):
        send_shapes = [jax.ShapeDtypeStruct((cap, half), BF16) for cap in caps]
        bufs = [pltpu.VMEM((cap + 4 * half, half), BF16) for cap in caps]
        sends = run_kernel(
            functools.partial(send_kernel, lay, half, caps),
            (table, own),
            [smem, vmem],
            send_shapes,
            [anywhere] * (ways - 1),
            scratch=bufs + [pltpu.SemaphoreType.DMA((ways - 1,))],
        )

        def step(turn, carried):
            state, image, sums, own, *sends = carried
            arrived = [cyclic(send, "sector", 1 + at) for at, send in enumerate(sends)]
            (site,) = run_kernel(
                functools.partial(site_kernel, lay, half),
                (table, own, left_one, right_one),
                [smem, packed, pair, pair],
                [block_f32],
                [square],
                flops=count * terms * 2 * flop,
                grid=(count,),
            )
            outs = run_kernel(
                functools.partial(hop_kernel, lay, half, caps),
                (table, turn.reshape(1), step_size, sums, own, *arrived, hop_first, hop_second, site, state, image),
                [smem, smem, smem, vmem] + [anywhere] * (ways + 5),
                [block_f32, block_f32, sums_shape, own_shape, *send_shapes],
                [anywhere, anywhere, vmem] + [anywhere] * ways,
                flops=count * hops * 2 * flop,
                scratch=[
                    pltpu.VMEM((full + sum(caps) + 4 * half, half), BF16),
                    pltpu.VMEM((hops, count, size, size), BF16),
                    pltpu.VMEM((hops, count, size, size), BF16),
                    pltpu.VMEM((count, size, size), F32),
                    pltpu.VMEM((count, size, size), F32),
                    pltpu.VMEM((count, size, size), F32),
                    pltpu.VMEM((ROWS, half), F32),
                    pltpu.SemaphoreType.DMA((6, max(ways, count))),
                    pltpu.SemaphoreType.DMA((3, count)),
                    pltpu.VMEM((full, half), BF16),
                    *bufs,
                ],
                reuse={4: 3, 7 + ways: 0, 8 + ways: 1},
            )
            return list(outs)

        zeros = jnp.zeros((8, LANES), F32)
        state, image, sums, *_ = lax.fori_loop(0, step_size.shape[1], step, [state, state, zeros, own, *sends])
        return state, image, sums

    state, image, sums = lax.switch(
        table[lay.plan],
        [functools.partial(update, caps) for caps in plans],
        state, own, table, step_size, left_one, right_one, hop_first, hop_second,
    )
    sums = lax.psum(sums, "sector")
    state, block = run_kernel(
        functools.partial(last_kernel, STEPS - 1),
        (step_size, sums, state, image),
        [smem, sums_spec, square, square],
        [block_f32, block_b16],
        [square, square],
        grid=(count,),
    )
    from_left = from_behind(block, "chain", 1)
    from_right = from_behind(block, "chain", -1)
    env_f32 = jax.ShapeDtypeStruct((terms, count, size, size), F32)
    merged_left, merged_right = run_kernel(
        functools.partial(merge_kernel, float(chi_total)),
        (from_left, from_right, left_next, right_next, left_one, right_one),
        [square, square, pair, pair, pair, pair],
        [env_f32, env_f32],
        [pair, pair],
        flops=count * terms * 4 * flop,
        grid=(count,),
    )
    return (state[None], merged_left[None], merged_right[None])


def solution(mesh):
    placed = (
        P("chain", "sector", None, None),
        P("chain", "sector"),
        P("chain", None),
        P("chain", None, "sector", None, None),
        P("chain", None, "sector", None, None),
        P("chain", None, "sector", None, None),
        P("chain", None, "sector", None, None),
        P(),
    )
    return jax.shard_map(
        on_device,
        mesh=mesh,
        in_specs=placed,
        out_specs=(
            P("chain", "sector", None, None),
            P("chain", None, "sector", None, None),
            P("chain", None, "sector", None, None),
        ),
        check_vma=False,
    )
```

```python
import functools

import jax
import jax.numpy as jnp
from jax import lax
from jax.experimental import pallas as pl
from jax.experimental.pallas import tpu as pltpu
from jax.sharding import PartitionSpec as P

LANES = 128
ROWS = 16
FAR = 1 << 20
F32 = jnp.float32
BF16 = jnp.bfloat16
I32 = jnp.int32
VMEM_BYTES = 20 * 1024 * 1024
PLANS = (
    (38, 22, 22),
    (44, 28, 22),
    (44, 22, 32),
    (50, 30, 28),
    (41, 38, 22),
    (56, 32, 34),
    (47, 44, 28),
    (50, 28, 44),
    (47, 40, 38),
    (59, 48, 48),
    (64, 64, 64),
)


def from_behind(value, axis, steps):
    count = lax.axis_size(axis)
    initial, last = (max(0, -steps), min(count, count - steps))
    return lax.ppermute(value, axis, [(source, source + steps) for source in range(initial, last)])


def partner(index, shift, ways):
    return index ^ shift if ways & (ways - 1) == 0 else (index + shift) % ways


def came_from(index, shift, ways):
    return index ^ shift if ways & (ways - 1) == 0 else (index + (ways - shift)) % ways


def exchange(value, axis, shift):
    count = lax.axis_size(axis)
    return lax.ppermute(value, axis, [(source, partner(source, shift, count)) for source in range(count)])


def dot(a, b):
    return jnp.dot(a, b, preferred_element_type=F32)


def mask_of(rank, size):
    rows = lax.broadcasted_iota(I32, (size, size), 0)
    cols = lax.broadcasted_iota(I32, (size, size), 1)
    return (rows < rank) & (cols < rank)


def weights(sums, step_now):
    total = jnp.sum(sums, axis=1, keepdims=True)
    self_dot, cross, image_dot = total[0:1], total[1:2], total[2:3]
    quotient = cross / self_dot
    state_resid = cross - quotient * self_dot
    resid_dot = image_dot - 2.0 * quotient * cross + quotient * quotient * self_dot
    new_dot = self_dot - 2.0 * step_now * state_resid + step_now * step_now * resid_dot
    norm = jnp.sqrt(new_dot)
    return (1.0 + step_now * quotient) / norm, -step_now / norm


def lane_sums(value):
    rows = jnp.sum(value, axis=0, keepdims=True)
    total = rows[:, 0:LANES]
    for at in range(LANES, rows.shape[1], LANES):
        total = total + rows[:, at : at + LANES]
    return total


def head_of(rows, room_ref):
    room_ref[...] = jnp.zeros_like(room_ref)
    for place, row in enumerate(rows):
        for part in range(3):
            now = row.astype(BF16).astype(F32)
            room_ref[3 * part + place : 3 * part + place + 1] = now
            row = row - now
    return room_ref[...].astype(BF16)


def rows_of_head(head, room_ref):
    room_ref[...] = head.astype(F32)
    return room_ref[0:3] + room_ref[3:6] + room_ref[6:9]


def kept_rows(rank):
    return (rank + (ROWS - 1)) & ~(ROWS - 1)


def packed_rows(rank, half):
    rows = kept_rows(rank)
    return jnp.where(rows <= half, rows, 3 * rows - 2 * half)


def at_rows(ref, start, rows):
    return ref.at[pl.ds(pl.multiple_of(start, ROWS), rows), :]


def quarters(value):
    half = value.shape[0] // 2
    return (
        value[:half, :half].astype(BF16),
        value[:half, half:].T.astype(BF16),
        value[half:, :half].astype(BF16),
        value[half:, half:].astype(BF16),
    )


def put_packed(ref, start, rank, parts):
    half = parts[0].shape[0]
    over = jnp.maximum(kept_rows(rank) - half, 0)
    for place, part in zip((0, half, half + over, half + 2 * over), parts):
        at_rows(ref, start + place, half)[...] = part


def get_packed(ref, start, rank, half):
    kept = kept_rows(rank)
    over = jnp.maximum(kept - half, 0)
    row = lax.broadcasted_iota(I32, (half, half), 0)

    def part(place, rows):
        value = at_rows(ref, start + place, half)[...].astype(F32)
        return jnp.where(row < rows, value, 0.0)

    first = part(0, kept).astype(BF16)
    second = part(half, over).T.astype(BF16)
    third = part(half + over, over).astype(BF16)
    fourth = part(half + 2 * over, over).astype(BF16)
    top = jnp.concatenate([first, second], axis=1)
    low = jnp.concatenate([third, fourth], axis=1)
    return jnp.concatenate([top, low], axis=0)


class Layout:
    def __init__(self, ways, count, hops):
        self.ways, self.count, self.hops = ways, count, hops
        self.plan = 0
        self.rank = 1
        self.send = self.rank + count
        self.shift = self.send + (ways - 1) * count
        self.start = self.shift + hops * count
        self.source_rank = self.start + hops * count
        self.size = self.source_rank + hops * count


def plan_kernel(lay, half, plans, me_ref, source_ref, *refs):
    ways, count, hops = lay.ways, lay.count, lay.hops
    rank_refs, (table_ref, need_ref, place_ref, all_ref) = refs[:ways], refs[ways:]
    me = me_ref[0]
    for at in range(ways * count * ways):
        need_ref[at] = 0
    for shift in range(ways):
        owner = came_from(me, shift, ways)
        for at in range(count):
            all_ref[owner * count + at] = rank_refs[shift][at]
    for hop in range(hops):
        for taker in range(ways):
            for at in range(count):
                need_ref[source_ref[hop, taker * count + at] * ways + taker] = 1
    largest = [jnp.int32(0)] * ways
    for owner in range(ways):
        for taker in range(ways):
            if owner == taker:
                continue
            shift = next(s for s in range(ways) if partner(owner, s, ways) == taker)
            used = jnp.int32(ROWS)
            for at in range(count):
                source = owner * count + at
                needed = need_ref[source * ways + taker] == 1
                rows = packed_rows(all_ref[source], half)

                @pl.when(owner == me)
                def _():
                    table_ref[lay.send + (shift - 1) * count + at] = jnp.where(needed, used, FAR)

                @pl.when(taker == me)
                def _():
                    place_ref[source] = used

                used = used + jnp.where(needed, rows, 0)
            largest[shift] = jnp.maximum(largest[shift], used)
    chosen = jnp.int32(len(plans) - 1)
    for index in reversed(range(len(plans) - 1)):
        fits = largest[1] <= plans[index][0]
        for shift in range(2, ways):
            fits = fits & (largest[shift] <= plans[index][shift - 1])
        chosen = jnp.where(fits, index, chosen)
    table_ref[lay.plan] = chosen
    for at in range(count):
        table_ref[lay.rank + at] = rank_refs[0][at]
        for hop in range(hops):
            source = source_ref[hop, me * count + at]
            owner = lax.div(source, count)
            here = owner == me
            slot = hop * count + at
            table_ref[lay.shift + slot] = me ^ owner if ways & (ways - 1) == 0 else (me + (ways - owner)) % ways
            table_ref[lay.start + slot] = jnp.where(here, (source - owner * count) * (4 * half), place_ref[source])
            table_ref[lay.source_rank + slot] = all_ref[source]


def fill_sends(lay, half, caps, table_ref, at, own_buf, send_bufs):
    packed = at_rows(own_buf, at * 4 * half, 4 * half)[...]
    for shift in range(1, lay.ways):
        start = jnp.minimum(table_ref[lay.send + (shift - 1) * lay.count + at], caps[shift - 1])
        at_rows(send_bufs[shift - 1], start, 4 * half)[...] = packed


def send_copies(send_bufs, send_outs, sems):
    return [
        pltpu.make_async_copy(buf.at[pl.ds(0, out.shape[0]), :], out, sems.at[at])
        for at, (buf, out) in enumerate(zip(send_bufs, send_outs))
    ]


def prepare_kernel(half, rank_ref, psi_ref, state_ref, image_ref, own_ref):
    rank = rank_ref[pl.program_id(0)]
    value = jnp.where(mask_of(rank, 2 * half), psi_ref[0], 0.0)
    state_ref[0] = value
    image_ref[0] = value
    put_packed(own_ref, 0, rank, quarters(value))


def send_kernel(lay, half, caps, table_ref, own_ref, sums_ref, *refs):
    sums_ref[...] = jnp.zeros_like(sums_ref)
    number = lay.ways - 1
    send_outs, send_bufs, sems = refs[:number], refs[number : 2 * number], refs[2 * number]
    for buf in send_bufs:
        buf[0:ROWS] = jnp.zeros((ROWS, half), BF16)

    @pl.loop(0, lay.count)
    def _(at):
        fill_sends(lay, half, caps, table_ref, at, own_ref, send_bufs)

    copies = send_copies(send_bufs, send_outs, sems)
    for copy in copies:
        copy.start()
    for copy in copies:
        copy.wait()


def two_sided(left_ref, right_ref, blocks):
    total = None
    for term, block in enumerate(blocks):
        part = dot(left_ref[term, 0], block).astype(BF16)
        now = dot(part, right_ref[term, 0])
        total = now if total is None else total + now
    return total


def site_kernel(lay, half, table_ref, own_ref, left_ref, right_ref, out_ref):
    block = get_packed(own_ref, 0, table_ref[lay.rank + pl.program_id(0)], half)
    out_ref[0] = two_sided(left_ref, right_ref, [block] * left_ref.shape[0])


def hop_kernel(lay, half, caps, table_ref, turn_ref, step_ref, sums_ref, *refs):
    ways, count, hops = lay.ways, lay.count, lay.hops
    size = 2 * half
    refs = list(refs)

    def take(number):
        out = refs[:number]
        del refs[:number]
        return out

    own_in, *packed_in = take(ways)
    left_in, right_in, site_in, state_in, image_in = take(5)
    state_out, image_out, sums_out = take(3)
    own_out, *send_outs = take(ways)
    pool, left, right, site, state, image, room, sems, out_sems = take(9)
    own_buf, *send_bufs = take(ways)

    places = [0, own_in.shape[0]]
    for cap in caps:
        places.append(places[-1] + cap)
    arrivals = [
        pltpu.make_async_copy(ref, pool.at[pl.ds(place, ref.shape[0]), :], sems.at[0, at])
        for at, (ref, place) in enumerate(zip([own_in, *packed_in], places))
    ]

    def inputs(at):
        return [
            pltpu.make_async_copy(left_in.at[:, at], left.at[:, at], sems.at[1, at]),
            pltpu.make_async_copy(right_in.at[:, at], right.at[:, at], sems.at[2, at]),
            pltpu.make_async_copy(site_in.at[at], site.at[at], sems.at[3, at]),
            pltpu.make_async_copy(state_in.at[at], state.at[at], sems.at[4, at]),
            pltpu.make_async_copy(image_in.at[at], image.at[at], sems.at[5, at]),
        ]

    def outputs(at):
        rows = pl.ds(pl.multiple_of(at * 4 * half, ROWS), 4 * half)
        return [
            pltpu.make_async_copy(state.at[at], state_out.at[at], out_sems.at[0, at]),
            pltpu.make_async_copy(image.at[at], image_out.at[at], out_sems.at[1, at]),
            pltpu.make_async_copy(own_buf.at[rows, :], own_out.at[rows, :], out_sems.at[2, at]),
        ]

    for copy in arrivals:
        copy.start()
    for at in range(count):
        for copy in inputs(at):
            copy.start()
    for copy in arrivals:
        copy.wait()

    sums = sums_ref[0:3]
    for place in places[1:ways]:
        sums = sums + rows_of_head(pool[place : place + ROWS], room)
    first = turn_ref[0] == 0
    keep, turn = weights(sums, step_ref[0, jnp.maximum(turn_ref[0] - 1, 0)])
    keep_state = jnp.where(first, 1.0, keep)
    keep_image = jnp.where(first, 0.0, keep)
    turn_state = jnp.where(first, 0.0, turn)
    turn_image = jnp.where(first, 1.0, turn)

    def sector(at, sums):
        for copy in inputs(at):
            copy.wait()
        total = site[at]
        for hop in range(hops):
            slot = hop * count + at
            shift = table_ref[lay.shift + slot]
            start = table_ref[lay.start + slot]
            for way in range(1, ways):
                start = start + jnp.where(shift == way, places[way], 0)
            block = get_packed(pool, start, table_ref[lay.source_rank + slot], half)
            part = dot(left[hop, at], block).astype(BF16)
            total = total + dot(part, right[hop, at])
        rank = table_ref[lay.rank + at]
        before = image[at]
        now = keep_state * state[at] + turn_state * before
        value = keep_image * before + turn_image * jnp.where(mask_of(rank, size), total, 0.0)
        state[at] = now
        image[at] = value
        put_packed(own_buf, at * 4 * half, rank, quarters(value))
        for copy in outputs(at):
            copy.start()
        fill_sends(lay, half, caps, table_ref, at, own_buf, send_bufs)
        return tuple(
            whole + lane_sums(part) for whole, part in zip(sums, (now * now, now * value, value * value))
        )

    rows = lax.fori_loop(0, count, sector, (jnp.zeros((1, LANES), F32),) * 3)
    head = head_of(rows, room)
    for buf in send_bufs:
        buf[0:ROWS] = head
    leaving = send_copies(send_bufs, send_outs, sems.at[0])
    for copy in leaving:
        copy.start()
    sums_out[...] = jnp.zeros_like(sums_out)
    for place, row in enumerate(rows):
        sums_out[place : place + 1] = row
    for copy in leaving:
        copy.wait()
    for at in range(count):
        for copy in outputs(at):
            copy.wait()


def last_kernel(step, step_ref, sums_ref, state_ref, image_ref, state_out, block_ref):
    keep, turn = weights(sums_ref[...], step_ref[0, step])

    @pl.loop(0, state_ref.shape[0])
    def _(at):
        state = keep * state_ref[at] + turn * image_ref[at]
        state_out[at] = state
        block_ref[at] = state.astype(BF16)


def merge_kernel(scale, from_left, from_right, left_next, right_next, left_own, right_own, left_out, right_out):
    a = from_left[0]
    b = from_right[0]
    a_turned = a.astype(F32).T.astype(BF16)
    b_turned = b.astype(F32).T.astype(BF16)
    for term in range(left_next.shape[0]):
        part = dot(a_turned, left_next[term, 0]).astype(BF16)
        left_out[term, 0] = left_own[term, 0].astype(F32) + scale * dot(part, a)
        part = dot(right_next[term, 0], b_turned).astype(BF16)
        right_out[term, 0] = right_own[term, 0].astype(F32) + scale * dot(b, part)


def run_kernel(body, args, in_specs, out_shape, out_specs, *, flops=0, grid=(), scratch=(), reuse=None):
    moved = sum(a.size * a.dtype.itemsize for a in args)
    moved += sum(s.size * s.dtype.itemsize for s in out_shape)
    return pl.pallas_call(
        body,
        grid=grid,
        in_specs=in_specs,
        out_specs=out_specs,
        out_shape=out_shape,
        scratch_shapes=list(scratch),
        input_output_aliases=reuse or {},
        compiler_params=pltpu.CompilerParams(vmem_limit_bytes=VMEM_BYTES),
        cost_estimate=pl.CostEstimate(flops=flops, bytes_accessed=moved, transcendentals=0),
    )(*args)


def on_device(psi, kept_rank, step_size, left_env, right_env, hop_left, hop_right, hop_source):
    count, size = psi.shape[1], psi.shape[2]
    half = size // 2
    terms, hops = left_env.shape[1], hop_left.shape[1]
    ways = lax.axis_size("sector")
    chi_total = count * ways * size
    lay = Layout(ways, count, hops)
    left_one, right_one = left_env[0], right_env[0]
    hop_first, hop_second = hop_left[0], hop_right[0]
    full = count * 4 * half
    plans = [tuple(ROWS * (full * part // (64 * ROWS)) + ROWS for part in plan) for plan in PLANS if len(plan) == ways - 1]
    if not plans:
        plans = [(full + ROWS,) * (ways - 1)]

    smem = pl.BlockSpec(memory_space=pltpu.SMEM)
    vmem = pl.BlockSpec(memory_space=pltpu.VMEM)
    anywhere = pl.BlockSpec(memory_space=pl.ANY)
    square = pl.BlockSpec((1, size, size), lambda t: (t, 0, 0))
    packed = pl.BlockSpec((4 * half, half), lambda t: (t, 0))
    pair = pl.BlockSpec((terms, 1, size, size), lambda t: (0, t, 0, 0))
    sums_spec = pl.BlockSpec((8, LANES), lambda t: (0, 0))
    block_f32 = jax.ShapeDtypeStruct((count, size, size), F32)
    block_b16 = jax.ShapeDtypeStruct((count, size, size), BF16)
    own_shape = jax.ShapeDtypeStruct((full, half), BF16)
    sums_shape = jax.ShapeDtypeStruct((8, LANES), F32)
    flop = 2 * size**3

    rank = kept_rank[0]
    ranks = [rank] + [exchange(rank, "sector", shift) for shift in range(1, ways)]
    left_next = from_behind(left_one, "chain", 1)
    right_next = from_behind(right_one, "chain", -1)
    state, image, own = run_kernel(
        functools.partial(prepare_kernel, half),
        (rank, psi[0]),
        [smem, square],
        [block_f32, block_f32, own_shape],
        [square, square, packed],
        grid=(count,),
    )
    me = lax.axis_index("sector").astype(I32).reshape(1)
    (table,) = run_kernel(
        functools.partial(plan_kernel, lay, half, plans),
        (me, hop_source, *ranks),
        [smem] * (2 + ways),
        [jax.ShapeDtypeStruct((lay.size,), I32)],
        [smem],
        scratch=[
            pltpu.SMEM((ways * count * ways,), I32),
            pltpu.SMEM((ways * count,), I32),
            pltpu.SMEM((ways * count,), I32),
        ],
    )

    def update(caps, state, image, own, table, step_size, left_one, right_one, hop_first, hop_second):
        send_shapes = [jax.ShapeDtypeStruct((cap, half), BF16) for cap in caps]
        bufs = [pltpu.VMEM((cap + 4 * half, half), BF16) for cap in caps]
        sums, *sends = run_kernel(
            functools.partial(send_kernel, lay, half, caps),
            (table, own),
            [smem, vmem],
            [sums_shape, *send_shapes],
            [vmem] + [anywhere] * (ways - 1),
            scratch=bufs + [pltpu.SemaphoreType.DMA((ways - 1,))],
        )

        def step(turn, carried):
            state, image, sums, own, *sends = carried
            arrived = [exchange(send, "sector", 1 + at) for at, send in enumerate(sends)]
            (site,) = run_kernel(
                functools.partial(site_kernel, lay, half),
                (table, own, left_one, right_one),
                [smem, packed, pair, pair],
                [block_f32],
                [square],
                flops=count * terms * 2 * flop,
                grid=(count,),
            )
            outs = run_kernel(
                functools.partial(hop_kernel, lay, half, caps),
                (table, turn.reshape(1), step_size, sums, own, *arrived, hop_first, hop_second, site, state, image),
                [smem, smem, smem, vmem] + [anywhere] * (ways + 5),
                [block_f32, block_f32, sums_shape, own_shape, *send_shapes],
                [anywhere, anywhere, vmem] + [anywhere] * ways,
                flops=count * hops * 2 * flop,
                scratch=[
                    pltpu.VMEM((full + sum(caps) + 4 * half, half), BF16),
                    pltpu.VMEM((hops, count, size, size), BF16),
                    pltpu.VMEM((hops, count, size, size), BF16),
                    pltpu.VMEM((count, size, size), F32),
                    pltpu.VMEM((count, size, size), F32),
                    pltpu.VMEM((count, size, size), F32),
                    pltpu.VMEM((ROWS, half), F32),
                    pltpu.SemaphoreType.DMA((6, max(ways, count))),
                    pltpu.SemaphoreType.DMA((3, count)),
                    pltpu.VMEM((full, half), BF16),
                    *bufs,
                ],
                reuse={4: 3, 7 + ways: 0, 8 + ways: 1},
            )
            return list(outs)

        state, image, sums, *_ = lax.fori_loop(0, step_size.shape[1], step, [state, image, sums, own, *sends])
        return state, image, sums

    state, image, sums = lax.switch(
        table[lay.plan],
        [functools.partial(update, caps) for caps in plans],
        state, image, own, table, step_size, left_one, right_one, hop_first, hop_second,
    )
    sums = lax.psum(sums, "sector")
    state, block = run_kernel(
        functools.partial(last_kernel, step_size.shape[1] - 1),
        (step_size, sums, state, image),
        [smem, vmem, vmem, vmem],
        [block_f32, block_b16],
        [vmem, vmem],
    )
    from_left = from_behind(block, "chain", 1)
    from_right = from_behind(block, "chain", -1)
    env_f32 = jax.ShapeDtypeStruct((terms, count, size, size), F32)
    merged_left, merged_right = run_kernel(
        functools.partial(merge_kernel, float(chi_total)),
        (from_left, from_right, left_next, right_next, left_one, right_one),
        [square, square, pair, pair, pair, pair],
        [env_f32, env_f32],
        [pair, pair],
        flops=count * terms * 4 * flop,
        grid=(count,),
    )
    return (state[None], merged_left[None], merged_right[None])


def solution(mesh):
    placed = (
        P("chain", "sector", None, None),
        P("chain", "sector"),
        P("chain", None),
        P("chain", None, "sector", None, None),
        P("chain", None, "sector", None, None),
        P("chain", None, "sector", None, None),
        P("chain", None, "sector", None, None),
        P(),
    )
    return jax.shard_map(
        on_device,
        mesh=mesh,
        in_specs=placed,
        out_specs=(
            P("chain", "sector", None, None),
            P("chain", None, "sector", None, None),
            P("chain", None, "sector", None, None),
        ),
        check_vma=False,
    )
```

```python
import functools
import math

import jax
import jax.numpy as jnp
from jax import lax
from jax.experimental import pallas as pl
from jax.experimental.pallas import tpu as pltpu
from jax.sharding import PartitionSpec as P

LANES = 128
ROWS = 16
FAR = 1 << 20
F32 = jnp.float32
BF16 = jnp.bfloat16
I32 = jnp.int32
VMEM_BYTES = 20 * 1024 * 1024
MOST_BYTES = 56 * 1024 * 1024
PLANS = (
    (48, 28, 22),
    (52, 20, 34),
    (48, 28, 32),
    (48, 38, 22),
    (56, 32, 34),
    (60, 22, 44),
    (56, 44, 28),
    (44, 38, 38),
    (60, 32, 48),
    (48, 48, 34),
    (60, 40, 54),
    (60, 52, 44),
    (64, 64, 64),
)


def from_behind(value, axis, steps):
    count = lax.axis_size(axis)
    initial, last = (max(0, -steps), min(count, count - steps))
    return lax.ppermute(value, axis, [(source, source + steps) for source in range(initial, last)])


def partner(index, shift, ways):
    return index ^ shift if ways & (ways - 1) == 0 else (index + shift) % ways


def came_from(index, shift, ways):
    return index ^ shift if ways & (ways - 1) == 0 else (index + (ways - shift)) % ways


def exchange(value, axis, shift):
    count = lax.axis_size(axis)
    return lax.ppermute(value, axis, [(source, partner(source, shift, count)) for source in range(count)])


def dot(a, b):
    return jnp.dot(a, b, preferred_element_type=F32)


def mask_of(rank, size):
    rows = lax.broadcasted_iota(I32, (size, size), 0)
    cols = lax.broadcasted_iota(I32, (size, size), 1)
    return (rows < rank) & (cols < rank)


def weights(sums, step_now):
    total = jnp.sum(sums, axis=1, keepdims=True)
    self_dot, cross, image_dot = total[0:1], total[1:2], total[2:3]
    quotient = cross / self_dot
    state_resid = cross - quotient * self_dot
    resid_dot = image_dot - 2.0 * quotient * cross + quotient * quotient * self_dot
    new_dot = self_dot - 2.0 * step_now * state_resid + step_now * step_now * resid_dot
    norm = jnp.sqrt(new_dot)
    return (1.0 + step_now * quotient) / norm, -step_now / norm


def lane_sums(value):
    rows = jnp.sum(value, axis=0, keepdims=True)
    total = rows[:, 0:LANES]
    for at in range(LANES, rows.shape[1], LANES):
        total = total + rows[:, at : at + LANES]
    return total


def head_of(rows, room_ref):
    room_ref[...] = jnp.zeros_like(room_ref)
    for place, row in enumerate(rows):
        for part in range(3):
            now = row.astype(BF16).astype(F32)
            room_ref[3 * part + place : 3 * part + place + 1] = now
            row = row - now
    return room_ref[...].astype(BF16)


def rows_of_head(head, room_ref):
    room_ref[...] = head.astype(F32)
    return room_ref[0:3] + room_ref[3:6] + room_ref[6:9]


def kept_rows(rank):
    return (rank + (ROWS - 1)) & ~(ROWS - 1)


def packed_rows(rank, half):
    rows = kept_rows(rank)
    return jnp.where(rows <= half, rows, 3 * rows - 2 * half)


def at_rows(ref, start, rows):
    return ref.at[pl.ds(pl.multiple_of(start, ROWS), rows), :]


def quarters(value):
    half = value.shape[0] // 2
    return (
        value[:half, :half].astype(BF16),
        value[:half, half:].T.astype(BF16),
        value[half:, :half].astype(BF16),
        value[half:, half:].astype(BF16),
    )


def put_packed(ref, start, rank, parts):
    half = parts[0].shape[0]
    over = jnp.maximum(kept_rows(rank) - half, 0)
    for place, part in zip((0, half, half + over, half + 2 * over), parts):
        at_rows(ref, start + place, half)[...] = part


def get_packed(ref, start, rank, half):
    kept = kept_rows(rank)
    over = jnp.maximum(kept - half, 0)
    row = lax.broadcasted_iota(I32, (half, half), 0)

    def part(place, rows):
        value = at_rows(ref, start + place, half)[...].astype(F32)
        return jnp.where(row < rows, value, 0.0)

    first = part(0, kept).astype(BF16)
    second = part(half, over).T.astype(BF16)
    third = part(half + over, over).astype(BF16)
    fourth = part(half + 2 * over, over).astype(BF16)
    top = jnp.concatenate([first, second], axis=1)
    low = jnp.concatenate([third, fourth], axis=1)
    return jnp.concatenate([top, low], axis=0)


class Layout:
    def __init__(self, ways, count, hops):
        self.ways, self.count, self.hops = ways, count, hops
        self.plan = 0
        self.rank = 1
        self.send = self.rank + count
        self.shift = self.send + (ways - 1) * count
        self.start = self.shift + hops * count
        self.source_rank = self.start + hops * count
        self.size = self.source_rank + hops * count


def plan_kernel(lay, half, plans, me_ref, source_ref, *refs):
    ways, count, hops = lay.ways, lay.count, lay.hops
    rank_refs, (table_ref, need_ref, place_ref, all_ref) = refs[:ways], refs[ways:]
    me = me_ref[0]
    for at in range(ways * count * ways):
        need_ref[at] = 0
    for shift in range(ways):
        owner = came_from(me, shift, ways)
        for at in range(count):
            all_ref[owner * count + at] = rank_refs[shift][at]
    for hop in range(hops):
        for taker in range(ways):
            for at in range(count):
                need_ref[source_ref[hop, taker * count + at] * ways + taker] = 1
    largest = [jnp.int32(0)] * ways
    for owner in range(ways):
        for taker in range(ways):
            if owner == taker:
                continue
            shift = next(s for s in range(ways) if partner(owner, s, ways) == taker)
            used = jnp.int32(ROWS)
            for at in range(count):
                source = owner * count + at
                needed = need_ref[source * ways + taker] == 1
                rows = packed_rows(all_ref[source], half)

                @pl.when(owner == me)
                def _():
                    table_ref[lay.send + (shift - 1) * count + at] = jnp.where(needed, used, FAR)

                @pl.when(taker == me)
                def _():
                    place_ref[source] = used

                used = used + jnp.where(needed, rows, 0)
            largest[shift] = jnp.maximum(largest[shift], used)
    chosen = jnp.int32(len(plans) - 1)
    for index in reversed(range(len(plans) - 1)):
        fits = largest[1] <= plans[index][0]
        for shift in range(2, ways):
            fits = fits & (largest[shift] <= plans[index][shift - 1])
        chosen = jnp.where(fits, index, chosen)
    table_ref[lay.plan] = chosen
    for at in range(count):
        table_ref[lay.rank + at] = rank_refs[0][at]
        for hop in range(hops):
            source = source_ref[hop, me * count + at]
            owner = lax.div(source, count)
            here = owner == me
            slot = hop * count + at
            table_ref[lay.shift + slot] = me ^ owner if ways & (ways - 1) == 0 else (me + (ways - owner)) % ways
            table_ref[lay.start + slot] = jnp.where(here, (source - owner * count) * (4 * half), place_ref[source])
            table_ref[lay.source_rank + slot] = all_ref[source]


def fill_send(lay, half, caps, table_ref, at, shift, own, send_bufs):
    start = jnp.minimum(table_ref[lay.send + (shift - 1) * lay.count + at], caps[shift - 1])
    at_rows(send_bufs[shift - 1], start, 4 * half)[...] = at_rows(own, at * 4 * half, 4 * half)[...]


def send_copies(send_bufs, send_outs, sems):
    return [
        pltpu.make_async_copy(buf.at[pl.ds(0, out.shape[0]), :], out, sems.at[at])
        for at, (buf, out) in enumerate(zip(send_bufs, send_outs))
    ]


def prepare_kernel(half, rank_ref, psi_in, state_ref, image_ref, own_ref, psi, sems):
    def arrival(at):
        return pltpu.make_async_copy(psi_in.at[at], psi.at[at], sems.at[at])

    count = psi.shape[0]
    for at in range(count):
        arrival(at).start()

    @pl.loop(0, count)
    def _(at):
        arrival(at).wait()
        rank = rank_ref[at]
        value = jnp.where(mask_of(rank, 2 * half), psi[at], 0.0)
        state_ref[at] = value
        image_ref[at] = value
        put_packed(own_ref, at * 4 * half, rank, quarters(value))


def send_kernel(lay, half, caps, table_ref, own_ref, sums_ref, *refs):
    sums_ref[...] = jnp.zeros_like(sums_ref)
    number = lay.ways - 1
    send_outs, send_bufs, sems = refs[:number], refs[number : 2 * number], refs[2 * number]
    copies = send_copies(send_bufs, send_outs, sems)
    for shift, copy in enumerate(copies, 1):
        send_bufs[shift - 1][0:ROWS] = jnp.zeros((ROWS, half), BF16)

        @pl.loop(0, lay.count)
        def _(at):
            fill_send(lay, half, caps, table_ref, at, shift, own_ref, send_bufs)

        copy.start()
    for copy in copies:
        copy.wait()


def site_kernel(lay, half, table_ref, own_ref, left_ref, right_ref, out_ref):
    block = get_packed(own_ref, 0, table_ref[lay.rank + pl.program_id(0)], half)
    part = dot(left_ref[0, 0], block).astype(BF16)
    total = dot(part, right_ref[0, 0])

    @pl.when(pl.program_id(1) == 0)
    def _():
        out_ref[0] = total

    @pl.when(pl.program_id(1) != 0)
    def _():
        out_ref[0] += total


def hop_kernel(lay, half, caps, table_ref, turn_ref, step_ref, sums_ref, *refs):
    ways, count, hops = lay.ways, lay.count, lay.hops
    size = 2 * half
    refs = list(refs)

    def take(number):
        out = refs[:number]
        del refs[:number]
        return out

    own_in, *packed_in = take(ways)
    left, right, site, state, image = take(5)
    state_out, image_out, sums_out = take(3)
    own_out, *send_outs = take(ways)
    pool, room, sems = take(3)
    send_bufs = take(ways - 1)

    places = [0, own_in.shape[0]]
    for cap in caps:
        places.append(places[-1] + cap)
    arrivals = [
        pltpu.make_async_copy(ref, pool.at[pl.ds(place, ref.shape[0]), :], sems.at[at])
        for at, (ref, place) in enumerate(zip([own_in, *packed_in], places))
    ]

    for copy in arrivals:
        copy.start()
    for copy in arrivals:
        copy.wait()

    sums = sums_ref[0:3]
    for place in places[1:ways]:
        sums = sums + rows_of_head(pool[place : place + ROWS], room)
    first = turn_ref[0] == 0
    keep, turn = weights(sums, step_ref[0, jnp.maximum(turn_ref[0] - 1, 0)])
    keep_state = jnp.where(first, 1.0, keep)
    keep_image = jnp.where(first, 0.0, keep)
    turn_state = jnp.where(first, 0.0, turn)
    turn_image = jnp.where(first, 1.0, turn)

    def sector(at, sums):
        total = site[at]
        for hop in range(hops):
            slot = hop * count + at
            shift = table_ref[lay.shift + slot]
            start = table_ref[lay.start + slot]
            for way in range(1, ways):
                start = start + jnp.where(shift == way, places[way], 0)
            block = get_packed(pool, start, table_ref[lay.source_rank + slot], half)
            part = dot(left[hop, at], block).astype(BF16)
            total = total + dot(part, right[hop, at])
        rank = table_ref[lay.rank + at]
        before = image[at]
        now = keep_state * state[at] + turn_state * before
        value = keep_image * before + turn_image * jnp.where(mask_of(rank, size), total, 0.0)
        state_out[at] = now
        image_out[at] = value
        put_packed(own_out, at * 4 * half, rank, quarters(value))
        for shift in range(1, ways):
            fill_send(lay, half, caps, table_ref, at, shift, own_out, send_bufs)
        return tuple(
            whole + lane_sums(part) for whole, part in zip(sums, (now * now, now * value, value * value))
        )

    rows = lax.fori_loop(0, count, sector, (jnp.zeros((1, LANES), F32),) * 3, unroll=2)
    head = head_of(rows, room)
    for buf in send_bufs:
        buf[0:ROWS] = head
    leaving = send_copies(send_bufs, send_outs, sems)
    for copy in leaving:
        copy.start()
    sums_out[...] = jnp.zeros_like(sums_out)
    for place, row in enumerate(rows):
        sums_out[place : place + 1] = row
    for copy in leaving:
        copy.wait()


def last_kernel(step, step_ref, state_ref, image_ref, *refs):
    *sums_refs, state_out, block_out, state_buf, block_buf, sems = refs
    keep, turn = weights(sum(ref[0:3] for ref in sums_refs), step_ref[0, step])

    def leaving(at):
        return [
            pltpu.make_async_copy(block_buf.at[at], block_out.at[at], sems.at[0, at]),
            pltpu.make_async_copy(state_buf.at[at], state_out.at[at], sems.at[1, at]),
        ]

    count = state_ref.shape[0]
    for at in range(count):
        state = keep * state_ref[at] + turn * image_ref[at]
        block_buf[at] = state.astype(BF16)
        state_buf[at] = state
        for copy in leaving(at):
            copy.start()
    for at in range(count):
        for copy in leaving(at):
            copy.wait()


def merge_kernel(scale, from_left, from_right, left_next, right_next, left_own, right_own, left_out, right_out, left_buf, right_buf, sems):
    terms, count = left_next.shape[:2]

    def leaving(at):
        return [
            pltpu.make_async_copy(left_buf.at[:, at], left_out.at[:, at], sems.at[0, at]),
            pltpu.make_async_copy(right_buf.at[:, at], right_out.at[:, at], sems.at[1, at]),
        ]

    def sector(at, done):
        a = from_left[at]
        b = from_right[at]
        a_turned = a.astype(F32).T.astype(BF16)
        b_turned = b.astype(F32).T.astype(BF16)
        lefts = [dot(a_turned, left_next[term, at]).astype(BF16) for term in range(terms)]
        rights = [dot(right_next[term, at], b_turned).astype(BF16) for term in range(terms)]
        for term in range(terms):
            left_buf[term, at] = left_own[term, at].astype(F32) + scale * dot(lefts[term], a)
            right_buf[term, at] = right_own[term, at].astype(F32) + scale * dot(b, rights[term])
        for copy in leaving(at):
            copy.start()
        return done

    lax.fori_loop(0, count, sector, 0, unroll=2)
    for at in range(count):
        for copy in leaving(at):
            copy.wait()


def run_kernel(body, args, in_specs, out_shape, out_specs, *, flops=0, grid=(), scratch=(), reuse=None, room=VMEM_BYTES):
    moved = sum(a.size * a.dtype.itemsize for a in args)
    moved += sum(math.prod(s.shape) * jnp.dtype(s.dtype).itemsize for s in out_shape)
    return pl.pallas_call(
        body,
        grid=grid,
        in_specs=in_specs,
        out_specs=out_specs,
        out_shape=out_shape,
        scratch_shapes=list(scratch),
        input_output_aliases=reuse or {},
        compiler_params=pltpu.CompilerParams(vmem_limit_bytes=room),
        cost_estimate=pl.CostEstimate(flops=flops, bytes_accessed=moved, transcendentals=0),
    )(*args)


def on_device(psi, kept_rank, step_size, left_env, right_env, hop_left, hop_right, hop_source):
    count, size = psi.shape[1], psi.shape[2]
    half = size // 2
    terms, hops = left_env.shape[1], hop_left.shape[1]
    ways = lax.axis_size("sector")
    chi_total = count * ways * size
    lay = Layout(ways, count, hops)
    left_one, right_one = left_env[0], right_env[0]
    hop_first, hop_second = hop_left[0], hop_right[0]
    full = count * 4 * half
    plans = [tuple(ROWS * (full * part // (64 * ROWS)) + ROWS for part in plan) for plan in PLANS if len(plan) == ways - 1]
    if not plans:
        plans = [(full + ROWS,) * (ways - 1)]

    smem = pl.BlockSpec(memory_space=pltpu.SMEM)
    vmem = pl.BlockSpec(memory_space=pltpu.VMEM)
    anywhere = pl.BlockSpec(memory_space=pl.ANY)
    square = pl.BlockSpec((1, size, size), lambda t, term: (t, 0, 0))
    packed = pl.BlockSpec((4 * half, half), lambda t, term: (t, 0))
    single = pl.BlockSpec((1, 1, size, size), lambda t, term: (term, t, 0, 0))
    block_f32 = jax.ShapeDtypeStruct((count, size, size), F32)
    here_f32 = pltpu.VMEM((count, size, size), F32)
    block_b16 = jax.ShapeDtypeStruct((count, size, size), BF16)
    here_own = pltpu.VMEM((full, half), BF16)
    sums_shape = jax.ShapeDtypeStruct((8, LANES), F32)
    flop = 2 * size**3

    rank = kept_rank[0]
    ranks = [rank] + [exchange(rank, "sector", shift) for shift in range(1, ways)]
    left_next = from_behind(left_one, "chain", 1)
    right_next = from_behind(right_one, "chain", -1)
    state, image, own = run_kernel(
        functools.partial(prepare_kernel, half),
        (rank, psi[0]),
        [smem, pl.BlockSpec(memory_space=pltpu.HBM)],
        [here_f32, here_f32, here_own],
        [vmem] * 3,
        scratch=[pltpu.VMEM((count, size, size), F32), pltpu.SemaphoreType.DMA((count,))],
        room=MOST_BYTES,
    )
    me = lax.axis_index("sector").astype(I32).reshape(1)
    (table,) = run_kernel(
        functools.partial(plan_kernel, lay, half, plans),
        (me, hop_source, *ranks),
        [smem] * (2 + ways),
        [jax.ShapeDtypeStruct((lay.size,), I32)],
        [smem],
        room=MOST_BYTES,
        scratch=[
            pltpu.SMEM((ways * count * ways,), I32),
            pltpu.SMEM((ways * count,), I32),
            pltpu.SMEM((ways * count,), I32),
        ],
    )

    def update(caps, state, image, own, table, step_size, left_one, right_one, hop_first, hop_second):
        send_shapes = [jax.ShapeDtypeStruct((cap, half), BF16) for cap in caps]
        bufs = [pltpu.VMEM((cap + 4 * half, half), BF16) for cap in caps]
        sums, *sends = run_kernel(
            functools.partial(send_kernel, lay, half, caps),
            (table, own),
            [smem, vmem],
            [sums_shape, *send_shapes],
            [vmem] + [anywhere] * (ways - 1),
            scratch=bufs + [pltpu.SemaphoreType.DMA((ways - 1,))],
        )

        def step(turn, carried):
            state, image, sums, own, *sends = carried
            arrived = [exchange(send, "sector", 1 + at) for at, send in enumerate(sends)]
            (site,) = run_kernel(
                functools.partial(site_kernel, lay, half),
                (table, own, left_one, right_one),
                [smem, packed, single, single],
                [block_f32],
                [square],
                flops=count * terms * 2 * flop,
                grid=(count, terms),
            )
            outs = run_kernel(
                functools.partial(hop_kernel, lay, half, caps),
                (table, turn.reshape(1), step_size, sums, own, *arrived, hop_first, hop_second, site, state, image),
                [smem, smem, smem, vmem] + [anywhere] * ways + [vmem] * 5,
                [here_f32, here_f32, sums_shape, here_own, *send_shapes],
                [vmem] * 4 + [anywhere] * (ways - 1),
                flops=count * hops * 2 * flop,
                scratch=[
                    pltpu.VMEM((full + sum(caps) + 4 * half, half), BF16),
                    pltpu.VMEM((ROWS, half), F32),
                    pltpu.SemaphoreType.DMA((ways,)),
                    *bufs,
                ],
                reuse={4: 3, 7 + ways: 0, 8 + ways: 1},
            )
            return list(outs)

        state, image, sums, *_ = lax.fori_loop(0, step_size.shape[1], step, [state, image, sums, own, *sends])
        return state, image, sums

    state, image, sums = lax.switch(
        table[lay.plan],
        [functools.partial(update, caps) for caps in plans],
        state, image, own, table, step_size, left_one, right_one, hop_first, hop_second,
    )
    every = [sums] + [exchange(sums, "sector", shift) for shift in range(1, ways)]
    state, block = run_kernel(
        functools.partial(last_kernel, step_size.shape[1] - 1),
        (step_size, state, image, *every),
        [smem] + [vmem] * (2 + ways),
        [block_f32, block_b16],
        [anywhere, anywhere],
        scratch=[
            pltpu.VMEM((count, size, size), F32),
            pltpu.VMEM((count, size, size), BF16),
            pltpu.SemaphoreType.DMA((2, count)),
        ],
    )
    from_left = from_behind(block, "chain", 1)
    from_right = from_behind(block, "chain", -1)
    env_f32 = jax.ShapeDtypeStruct((terms, count, size, size), F32)
    merged_left, merged_right = run_kernel(
        functools.partial(merge_kernel, float(chi_total)),
        (from_left, from_right, left_next, right_next, left_one, right_one),
        [vmem] * 6,
        [env_f32, env_f32],
        [anywhere, anywhere],
        flops=count * terms * 4 * flop,
        scratch=[
            pltpu.VMEM((terms, count, size, size), F32),
            pltpu.VMEM((terms, count, size, size), F32),
            pltpu.SemaphoreType.DMA((2, count)),
        ],
    )
    return (state[None], merged_left[None], merged_right[None])


def solution(mesh):
    placed = (
        P("chain", "sector", None, None),
        P("chain", "sector"),
        P("chain", None),
        P("chain", None, "sector", None, None),
        P("chain", None, "sector", None, None),
        P("chain", None, "sector", None, None),
        P("chain", None, "sector", None, None),
        P(),
    )
    return jax.shard_map(
        on_device,
        mesh=mesh,
        in_specs=placed,
        out_specs=(
            P("chain", "sector", None, None),
            P("chain", None, "sector", None, None),
            P("chain", None, "sector", None, None),
        ),
        check_vma=False,
    )
```

```python
import functools
import math

import jax
import jax.numpy as jnp
from jax import lax
from jax.experimental import pallas as pl
from jax.experimental.pallas import tpu as pltpu
from jax.sharding import PartitionSpec as P

LANES = 128
ROWS = 16
FAR = 1 << 20
F32 = jnp.float32
BF16 = jnp.bfloat16
I32 = jnp.int32
VMEM_BYTES = 20 * 1024 * 1024
MOST_BYTES = 56 * 1024 * 1024
PLANS = (
    (48, 28, 22),
    (52, 20, 34),
    (44, 38, 22),
    (48, 28, 32),
    (60, 32, 28),
    (56, 26, 38),
    (52, 34, 34),
    (60, 22, 46),
    (48, 44, 28),
    (44, 38, 38),
    (52, 32, 48),
    (60, 48, 32),
    (60, 44, 44),
    (36, 34, 56),
    (44, 56, 34),
    (36, 50, 50),
    (64, 64, 64),
)


def from_behind(value, axis, steps):
    count = lax.axis_size(axis)
    initial, last = (max(0, -steps), min(count, count - steps))
    return lax.ppermute(value, axis, [(source, source + steps) for source in range(initial, last)])


def partner(index, shift, ways):
    return index ^ shift if ways & (ways - 1) == 0 else (index + shift) % ways


def came_from(index, shift, ways):
    return index ^ shift if ways & (ways - 1) == 0 else (index + (ways - shift)) % ways


def exchange(value, axis, shift):
    count = lax.axis_size(axis)
    return lax.ppermute(value, axis, [(source, partner(source, shift, count)) for source in range(count)])


def dot(a, b):
    return jnp.dot(a, b, preferred_element_type=F32)


def mask_of(rank, size):
    rows = lax.broadcasted_iota(I32, (size, size), 0)
    cols = lax.broadcasted_iota(I32, (size, size), 1)
    return (rows < rank) & (cols < rank)


def weights(sums, step_now):
    total = jnp.sum(sums, axis=1, keepdims=True)
    self_dot, cross, image_dot = total[0:1], total[1:2], total[2:3]
    quotient = cross / self_dot
    state_resid = cross - quotient * self_dot
    resid_dot = image_dot - 2.0 * quotient * cross + quotient * quotient * self_dot
    new_dot = self_dot - 2.0 * step_now * state_resid + step_now * step_now * resid_dot
    norm = jnp.sqrt(new_dot)
    return (1.0 + step_now * quotient) / norm, -step_now / norm


def lane_sums(value):
    rows = jnp.sum(value, axis=0, keepdims=True)
    total = rows[:, 0:LANES]
    for at in range(LANES, rows.shape[1], LANES):
        total = total + rows[:, at : at + LANES]
    return total


def head_of(rows, room_ref):
    room_ref[...] = jnp.zeros_like(room_ref)
    for place, row in enumerate(rows):
        for part in range(3):
            now = row.astype(BF16).astype(F32)
            room_ref[3 * part + place : 3 * part + place + 1] = now
            row = row - now
    return room_ref[...].astype(BF16)


def rows_of_head(head, room_ref):
    room_ref[...] = head.astype(F32)
    return room_ref[0:3] + room_ref[3:6] + room_ref[6:9]


def kept_rows(rank):
    return (rank + (ROWS - 1)) & ~(ROWS - 1)


def packed_rows(rank, half):
    rows = kept_rows(rank)
    return jnp.where(rows <= half, rows, 3 * rows - 2 * half)


def at_rows(ref, start, rows):
    return ref.at[pl.ds(pl.multiple_of(start, ROWS), rows), :]


def quarters(value):
    half = value.shape[0] // 2
    return (
        value[:half, :half].astype(BF16),
        value[:half, half:].T.astype(BF16),
        value[half:, :half].astype(BF16),
        value[half:, half:].astype(BF16),
    )


def put_packed(ref, start, rank, parts):
    half = parts[0].shape[0]
    over = jnp.maximum(kept_rows(rank) - half, 0)
    for place, part in zip((0, half, half + over, half + 2 * over), parts):
        at_rows(ref, start + place, half)[...] = part


def get_packed(ref, start, rank, half):
    kept = kept_rows(rank)
    over = jnp.maximum(kept - half, 0)
    row = lax.broadcasted_iota(I32, (half, half), 0)

    def part(place, rows):
        value = at_rows(ref, start + place, half)[...].astype(F32)
        return jnp.where(row < rows, value, 0.0)

    first = part(0, kept).astype(BF16)
    second = part(half, over).T.astype(BF16)
    third = part(half + over, over).astype(BF16)
    fourth = part(half + 2 * over, over).astype(BF16)
    top = jnp.concatenate([first, second], axis=1)
    low = jnp.concatenate([third, fourth], axis=1)
    return jnp.concatenate([top, low], axis=0)


class Layout:
    def __init__(self, ways, count, hops):
        self.ways, self.count, self.hops = ways, count, hops
        self.plan = 0
        self.rank = 1
        self.send = self.rank + count
        self.shift = self.send + (ways - 1) * count
        self.start = self.shift + hops * count
        self.source_rank = self.start + hops * count
        self.size = self.source_rank + hops * count


def plan_kernel(lay, half, plans, me_ref, source_ref, *refs):
    ways, count, hops = lay.ways, lay.count, lay.hops
    rank_refs, (table_ref, need_ref, place_ref, all_ref) = refs[:ways], refs[ways:]
    me = me_ref[0]
    for at in range(ways * count * ways):
        need_ref[at] = 0
    for shift in range(ways):
        owner = came_from(me, shift, ways)
        for at in range(count):
            all_ref[owner * count + at] = rank_refs[shift][at]
    for hop in range(hops):
        for taker in range(ways):
            for at in range(count):
                need_ref[source_ref[hop, taker * count + at] * ways + taker] = 1
    largest = [jnp.int32(0)] * ways
    for owner in range(ways):
        for taker in range(ways):
            if owner == taker:
                continue
            shift = next(s for s in range(ways) if partner(owner, s, ways) == taker)
            used = jnp.int32(ROWS)
            for at in range(count):
                source = owner * count + at
                needed = need_ref[source * ways + taker] == 1
                rows = packed_rows(all_ref[source], half)

                @pl.when(owner == me)
                def _():
                    table_ref[lay.send + (shift - 1) * count + at] = jnp.where(needed, used, FAR)

                @pl.when(taker == me)
                def _():
                    place_ref[source] = used

                used = used + jnp.where(needed, rows, 0)
            largest[shift] = jnp.maximum(largest[shift], used)
    chosen = jnp.int32(len(plans) - 1)
    for index in reversed(range(len(plans) - 1)):
        fits = largest[1] <= plans[index][0]
        for shift in range(2, ways):
            fits = fits & (largest[shift] <= plans[index][shift - 1])
        chosen = jnp.where(fits, index, chosen)
    table_ref[lay.plan] = len(plans) - 1 - chosen
    for at in range(count):
        table_ref[lay.rank + at] = rank_refs[0][at]
        for hop in range(hops):
            source = source_ref[hop, me * count + at]
            owner = lax.div(source, count)
            here = owner == me
            slot = hop * count + at
            table_ref[lay.shift + slot] = me ^ owner if ways & (ways - 1) == 0 else (me + (ways - owner)) % ways
            table_ref[lay.start + slot] = jnp.where(here, (source - owner * count) * (4 * half), place_ref[source])
            table_ref[lay.source_rank + slot] = all_ref[source]


def fill_send(lay, half, caps, table_ref, at, shift, own, send_bufs):
    start = jnp.minimum(table_ref[lay.send + (shift - 1) * lay.count + at], caps[shift - 1])
    at_rows(send_bufs[shift - 1], start, 4 * half)[...] = at_rows(own, at * 4 * half, 4 * half)[...]


def send_copies(send_bufs, send_outs, sems):
    return [
        pltpu.make_async_copy(buf.at[pl.ds(0, out.shape[0]), :], out, sems.at[at])
        for at, (buf, out) in enumerate(zip(send_bufs, send_outs))
    ]


def prepare_kernel(half, rank_ref, psi_in, state_ref, image_ref, own_ref, psi, sems):
    def arrival(at):
        return pltpu.make_async_copy(psi_in.at[at], psi.at[at], sems.at[at])

    count = psi.shape[0]
    for at in range(count):
        arrival(at).start()

    @pl.loop(0, count)
    def _(at):
        arrival(at).wait()
        rank = rank_ref[at]
        value = jnp.where(mask_of(rank, 2 * half), psi[at], 0.0)
        state_ref[at] = value
        image_ref[at] = value
        put_packed(own_ref, at * 4 * half, rank, quarters(value))


def send_kernel(lay, half, caps, table_ref, own_ref, sums_ref, *refs):
    sums_ref[...] = jnp.zeros_like(sums_ref)
    number = lay.ways - 1
    send_outs, send_bufs, sems = refs[:number], refs[number : 2 * number], refs[2 * number]
    copies = send_copies(send_bufs, send_outs, sems)
    for shift, copy in enumerate(copies, 1):
        send_bufs[shift - 1][0:ROWS] = jnp.zeros((ROWS, half), BF16)

        @pl.loop(0, lay.count)
        def _(at):
            fill_send(lay, half, caps, table_ref, at, shift, own_ref, send_bufs)

        copy.start()
    for copy in copies:
        copy.wait()


def site_kernel(lay, half, table_ref, own_ref, left_ref, right_ref, out_ref):
    block = get_packed(own_ref, 0, table_ref[lay.rank + pl.program_id(0)], half)
    part = dot(left_ref[0, 0], block).astype(BF16)
    total = dot(part, right_ref[0, 0])

    @pl.when(pl.program_id(1) == 0)
    def _():
        out_ref[0] = total

    @pl.when(pl.program_id(1) != 0)
    def _():
        out_ref[0] += total


def hop_kernel(lay, half, caps, table_ref, turn_ref, step_ref, sums_ref, *refs):
    ways, count, hops = lay.ways, lay.count, lay.hops
    size = 2 * half
    refs = list(refs)

    def take(number):
        out = refs[:number]
        del refs[:number]
        return out

    own_in, *packed_in = take(ways)
    left, right, site, state, image = take(5)
    state_out, image_out, sums_out = take(3)
    own_out, *send_outs = take(ways)
    pool, room, sems = take(3)
    send_bufs = take(ways - 1)

    places = [0, own_in.shape[0]]
    for cap in caps:
        places.append(places[-1] + cap)
    arrivals = [
        pltpu.make_async_copy(ref, pool.at[pl.ds(place, ref.shape[0]), :], sems.at[at])
        for at, (ref, place) in enumerate(zip([own_in, *packed_in], places))
    ]

    for copy in arrivals:
        copy.start()
    for copy in arrivals:
        copy.wait()

    sums = sums_ref[0:3]
    for place in places[1:ways]:
        sums = sums + rows_of_head(pool[place : place + ROWS], room)
    first = turn_ref[0] == 0
    keep, turn = weights(sums, step_ref[0, jnp.maximum(turn_ref[0] - 1, 0)])
    keep_state = jnp.where(first, 1.0, keep)
    keep_image = jnp.where(first, 0.0, keep)
    turn_state = jnp.where(first, 0.0, turn)
    turn_image = jnp.where(first, 1.0, turn)

    def sector(at, sums):
        total = site[at]
        for hop in range(hops):
            slot = hop * count + at
            shift = table_ref[lay.shift + slot]
            start = table_ref[lay.start + slot]
            for way in range(1, ways):
                start = start + jnp.where(shift == way, places[way], 0)
            block = get_packed(pool, start, table_ref[lay.source_rank + slot], half)
            part = dot(left[hop, at], block).astype(BF16)
            total = total + dot(part, right[hop, at])
        rank = table_ref[lay.rank + at]
        before = image[at]
        now = keep_state * state[at] + turn_state * before
        value = keep_image * before + turn_image * jnp.where(mask_of(rank, size), total, 0.0)
        state_out[at] = now
        image_out[at] = value
        put_packed(own_out, at * 4 * half, rank, quarters(value))
        for shift in range(1, ways):
            fill_send(lay, half, caps, table_ref, at, shift, own_out, send_bufs)
        return tuple(
            whole + lane_sums(part) for whole, part in zip(sums, (now * now, now * value, value * value))
        )

    rows = lax.fori_loop(0, count, sector, (jnp.zeros((1, LANES), F32),) * 3, unroll=2)
    head = head_of(rows, room)
    for buf in send_bufs:
        buf[0:ROWS] = head
    leaving = send_copies(send_bufs, send_outs, sems)
    for copy in leaving:
        copy.start()
    sums_out[...] = jnp.zeros_like(sums_out)
    for place, row in enumerate(rows):
        sums_out[place : place + 1] = row
    for copy in leaving:
        copy.wait()


def last_kernel(step, step_ref, state_ref, image_ref, *refs):
    *sums_refs, block_out, weight_out = refs
    keep, turn = weights(sum(ref[0:3] for ref in sums_refs), step_ref[0, step])
    weight_out[0:1] = jnp.broadcast_to(keep, (1, LANES))
    weight_out[1:2] = jnp.broadcast_to(turn, (1, LANES))
    for at in range(state_ref.shape[0]):
        block_out[at] = (keep * state_ref[at] + turn * image_ref[at]).astype(BF16)


def state_kernel(weight_ref, state_ref, image_ref, *refs):
    number = (len(refs) - 2) // 2
    ins, state_out, outs, sems = refs[:number], refs[number], refs[number + 1 : -1], refs[-1]
    copies = [pltpu.make_async_copy(ref, out, sems.at[at]) for at, (ref, out) in enumerate(zip(ins, outs))]
    for copy in copies:
        copy.start()
    keep, turn = weight_ref[0:1, 0:1], weight_ref[1:2, 0:1]
    for at in range(state_ref.shape[0]):
        state_out[at] = keep * state_ref[at] + turn * image_ref[at]
    for copy in copies:
        copy.wait()


def merge_kernel(scale, from_left, from_right, left_next, right_next, left_own, right_own, left_out, right_out, left_buf, right_buf, sems):
    terms, count = left_next.shape[:2]

    def leaving(term, at):
        return (
            pltpu.make_async_copy(left_buf.at[term, at], left_out.at[term, at], sems.at[0, term, at]),
            pltpu.make_async_copy(right_buf.at[term, at], right_out.at[term, at], sems.at[1, term, at]),
        )

    def sector(at, done):
        a = from_left[at]
        b = from_right[at]
        a_turned = a.astype(F32).T.astype(BF16)
        b_turned = b.astype(F32).T.astype(BF16)
        lefts = [dot(a_turned, left_next[term, at]).astype(BF16) for term in range(terms)]
        rights = [dot(right_next[term, at], b_turned).astype(BF16) for term in range(terms)]
        for term in range(terms):
            left_copy, right_copy = leaving(term, at)
            left_buf[term, at] = left_own[term, at].astype(F32) + scale * dot(lefts[term], a)
            left_copy.start()
            right_buf[term, at] = right_own[term, at].astype(F32) + scale * dot(b, rights[term])
            right_copy.start()
        return done

    lax.fori_loop(0, count, sector, 0, unroll=2)
    for term in range(terms):
        for at in range(count):
            for copy in leaving(term, at):
                copy.wait()


def run_kernel(body, args, in_specs, out_shape, out_specs, *, flops=0, grid=(), scratch=(), reuse=None, room=VMEM_BYTES):
    moved = sum(a.size * a.dtype.itemsize for a in args)
    moved += sum(math.prod(s.shape) * jnp.dtype(s.dtype).itemsize for s in out_shape)
    return pl.pallas_call(
        body,
        grid=grid,
        in_specs=in_specs,
        out_specs=out_specs,
        out_shape=out_shape,
        scratch_shapes=list(scratch),
        input_output_aliases=reuse or {},
        compiler_params=pltpu.CompilerParams(vmem_limit_bytes=room),
        cost_estimate=pl.CostEstimate(flops=flops, bytes_accessed=moved, transcendentals=0),
    )(*args)


def on_device(psi, kept_rank, step_size, left_env, right_env, hop_left, hop_right, hop_source):
    count, size = psi.shape[1], psi.shape[2]
    half = size // 2
    terms, hops = left_env.shape[1], hop_left.shape[1]
    ways = lax.axis_size("sector")
    chi_total = count * ways * size
    lay = Layout(ways, count, hops)
    left_one, right_one = left_env[0], right_env[0]
    hop_first, hop_second = hop_left[0], hop_right[0]
    full = count * 4 * half
    plans = [tuple(ROWS * (full * part // (64 * ROWS)) + ROWS for part in plan) for plan in PLANS if len(plan) == ways - 1]
    if not plans:
        plans = [(full + ROWS,) * (ways - 1)]

    smem = pl.BlockSpec(memory_space=pltpu.SMEM)
    vmem = pl.BlockSpec(memory_space=pltpu.VMEM)
    anywhere = pl.BlockSpec(memory_space=pl.ANY)
    square = pl.BlockSpec((1, size, size), lambda t, term: (t, 0, 0))
    packed = pl.BlockSpec((4 * half, half), lambda t, term: (t, 0))
    single = pl.BlockSpec((1, 1, size, size), lambda t, term: (term, t, 0, 0))
    block_f32 = jax.ShapeDtypeStruct((count, size, size), F32)
    here_f32 = pltpu.VMEM((count, size, size), F32)
    block_b16 = jax.ShapeDtypeStruct((count, size, size), BF16)
    here_own = pltpu.VMEM((full, half), BF16)
    sums_shape = jax.ShapeDtypeStruct((8, LANES), F32)
    flop = 2 * size**3

    rank = kept_rank[0]
    ranks = [rank] + [exchange(rank, "sector", shift) for shift in range(1, ways)]
    left_next = from_behind(left_one, "chain", 1)
    right_next = from_behind(right_one, "chain", -1)
    state, image, own = run_kernel(
        functools.partial(prepare_kernel, half),
        (rank, psi[0]),
        [smem, pl.BlockSpec(memory_space=pltpu.HBM)],
        [here_f32, here_f32, here_own],
        [vmem] * 3,
        scratch=[pltpu.VMEM((count, size, size), F32), pltpu.SemaphoreType.DMA((count,))],
        room=MOST_BYTES,
    )
    me = lax.axis_index("sector").astype(I32).reshape(1)
    (table,) = run_kernel(
        functools.partial(plan_kernel, lay, half, plans),
        (me, hop_source, *ranks),
        [smem] * (2 + ways),
        [jax.ShapeDtypeStruct((lay.size,), I32)],
        [smem],
        room=MOST_BYTES,
        scratch=[
            pltpu.SMEM((ways * count * ways,), I32),
            pltpu.SMEM((ways * count,), I32),
            pltpu.SMEM((ways * count,), I32),
        ],
    )

    def update(caps, state, image, own, table, step_size, left_one, right_one, hop_first, hop_second):
        send_shapes = [jax.ShapeDtypeStruct((cap, half), BF16) for cap in caps]
        bufs = [pltpu.VMEM((cap + 4 * half, half), BF16) for cap in caps]
        sums, *sends = run_kernel(
            functools.partial(send_kernel, lay, half, caps),
            (table, own),
            [smem, vmem],
            [sums_shape, *send_shapes],
            [vmem] + [anywhere] * (ways - 1),
            scratch=bufs + [pltpu.SemaphoreType.DMA((ways - 1,))],
        )

        def step(turn, carried):
            state, image, sums, own, *sends = carried
            arrived = [exchange(send, "sector", 1 + at) for at, send in enumerate(sends)]
            (site,) = run_kernel(
                functools.partial(site_kernel, lay, half),
                (table, own, left_one, right_one),
                [smem, packed, single, single],
                [block_f32],
                [square],
                flops=count * terms * 2 * flop,
                grid=(count, terms),
            )
            outs = run_kernel(
                functools.partial(hop_kernel, lay, half, caps),
                (table, turn.reshape(1), step_size, sums, own, *arrived, hop_first, hop_second, site, state, image),
                [smem, smem, smem, vmem] + [anywhere] * ways + [vmem] * 5,
                [here_f32, here_f32, sums_shape, here_own, *send_shapes],
                [vmem] * 4 + [anywhere] * (ways - 1),
                flops=count * hops * 2 * flop,
                scratch=[
                    pltpu.VMEM((full + sum(caps) + 4 * half, half), BF16),
                    pltpu.VMEM((ROWS, half), F32),
                    pltpu.SemaphoreType.DMA((ways,)),
                    *bufs,
                ],
                reuse={4: 3, 7 + ways: 0, 8 + ways: 1},
            )
            return list(outs)

        state, image, sums, *_ = lax.fori_loop(0, step_size.shape[1], step, [state, image, sums, own, *sends])
        return state, image, sums

    state, image, sums = lax.switch(
        table[lay.plan],
        [functools.partial(update, caps) for caps in reversed(plans)],
        state, image, own, table, step_size, left_one, right_one, hop_first, hop_second,
    )
    every = [sums] + [exchange(sums, "sector", shift) for shift in range(1, ways)]
    block, weight = run_kernel(
        functools.partial(last_kernel, step_size.shape[1] - 1),
        (step_size, state, image, *every),
        [smem] + [vmem] * (2 + ways),
        [block_b16, pltpu.VMEM((8, LANES), F32)],
        [vmem, vmem],
    )
    from_left = from_behind(block, "chain", 1)
    from_right = from_behind(block, "chain", -1)
    envs = (left_next, right_next, left_one, right_one)
    state, *envs = run_kernel(
        state_kernel,
        (weight, state, image, *envs),
        [vmem] * 3 + [anywhere] * len(envs),
        [block_f32] + [pltpu.VMEM(env.shape, BF16) for env in envs],
        [vmem] * (1 + len(envs)),
        scratch=[pltpu.SemaphoreType.DMA((len(envs),))],
    )
    env_f32 = jax.ShapeDtypeStruct((terms, count, size, size), F32)
    merged_left, merged_right = run_kernel(
        functools.partial(merge_kernel, float(chi_total)),
        (from_left, from_right, *envs),
        [vmem] * 6,
        [env_f32, env_f32],
        [anywhere, anywhere],
        flops=count * terms * 4 * flop,
        scratch=[
            pltpu.VMEM((terms, count, size, size), F32),
            pltpu.VMEM((terms, count, size, size), F32),
            pltpu.SemaphoreType.DMA((2, terms, count)),
        ],
    )
    return (state[None], merged_left[None], merged_right[None])


def solution(mesh):
    placed = (
        P("chain", "sector", None, None),
        P("chain", "sector"),
        P("chain", None),
        P("chain", None, "sector", None, None),
        P("chain", None, "sector", None, None),
        P("chain", None, "sector", None, None),
        P("chain", None, "sector", None, None),
        P(),
    )
    return jax.shard_map(
        on_device,
        mesh=mesh,
        in_specs=placed,
        out_specs=(
            P("chain", "sector", None, None),
            P("chain", None, "sector", None, None),
            P("chain", None, "sector", None, None),
        ),
        check_vma=False,
    )
```

```python
import functools
import math

import jax
import jax.numpy as jnp
from jax import lax
from jax.experimental import pallas as pl
from jax.experimental.pallas import tpu as pltpu
from jax.sharding import PartitionSpec as P

LANES = 128
ROWS = 16
FAR = 1 << 20
F32 = jnp.float32
BF16 = jnp.bfloat16
I32 = jnp.int32
VMEM_BYTES = 20 * 1024 * 1024
MOST_BYTES = 56 * 1024 * 1024
PLANS = (
    (48, 28, 22),
    (52, 20, 34),
    (44, 38, 22),
    (48, 28, 32),
    (60, 32, 28),
    (56, 26, 38),
    (52, 34, 34),
    (60, 22, 46),
    (48, 44, 28),
    (44, 38, 38),
    (52, 32, 48),
    (60, 48, 32),
    (60, 44, 44),
    (36, 34, 56),
    (44, 56, 34),
    (36, 50, 50),
    (64, 64, 64),
)


def from_behind(value, axis, steps):
    count = lax.axis_size(axis)
    initial, last = (max(0, -steps), min(count, count - steps))
    return lax.ppermute(value, axis, [(source, source + steps) for source in range(initial, last)])


def partner(index, shift, ways):
    return index ^ shift if ways & (ways - 1) == 0 else (index + shift) % ways


def came_from(index, shift, ways):
    return index ^ shift if ways & (ways - 1) == 0 else (index + (ways - shift)) % ways


def exchange(value, axis, shift):
    count = lax.axis_size(axis)
    return lax.ppermute(value, axis, [(source, partner(source, shift, count)) for source in range(count)])


def dot(a, b):
    return jnp.dot(a, b, preferred_element_type=F32)


def mask_of(rank, size):
    rows = lax.broadcasted_iota(I32, (size, size), 0)
    cols = lax.broadcasted_iota(I32, (size, size), 1)
    return (rows < rank) & (cols < rank)


def weights(sums, step_now):
    total = jnp.sum(sums, axis=1, keepdims=True)
    self_dot, cross, image_dot = total[0:1], total[1:2], total[2:3]
    quotient = cross / self_dot
    state_resid = cross - quotient * self_dot
    resid_dot = image_dot - 2.0 * quotient * cross + quotient * quotient * self_dot
    new_dot = self_dot - 2.0 * step_now * state_resid + step_now * step_now * resid_dot
    norm = jnp.sqrt(new_dot)
    return (1.0 + step_now * quotient) / norm, -step_now / norm


def lane_sums(value):
    rows = jnp.sum(value, axis=0, keepdims=True)
    total = rows[:, 0:LANES]
    for at in range(LANES, rows.shape[1], LANES):
        total = total + rows[:, at : at + LANES]
    return total


def head_of(rows, room_ref):
    room_ref[...] = jnp.zeros_like(room_ref)
    for place, row in enumerate(rows):
        for part in range(3):
            now = row.astype(BF16).astype(F32)
            room_ref[3 * part + place : 3 * part + place + 1] = now
            row = row - now
    return room_ref[...].astype(BF16)


def rows_of_head(head, room_ref):
    room_ref[...] = head.astype(F32)
    return room_ref[0:3] + room_ref[3:6] + room_ref[6:9]


def kept_rows(rank):
    return (rank + (ROWS - 1)) & ~(ROWS - 1)


def packed_rows(rank, half):
    rows = kept_rows(rank)
    return jnp.where(rows <= half, rows, 3 * rows - 2 * half)


def at_rows(ref, start, rows):
    return ref.at[pl.ds(pl.multiple_of(start, ROWS), rows), :]


def quarters(value):
    half = value.shape[0] // 2
    return (
        value[:half, :half].astype(BF16),
        value[:half, half:].T.astype(BF16),
        value[half:, :half].astype(BF16),
        value[half:, half:].astype(BF16),
    )


def put_packed(ref, start, rank, parts):
    half = parts[0].shape[0]
    over = jnp.maximum(kept_rows(rank) - half, 0)
    for place, part in zip((0, half, half + over, half + 2 * over), parts):
        at_rows(ref, start + place, half)[...] = part


def get_packed(ref, start, rank, half):
    kept = kept_rows(rank)
    over = jnp.maximum(kept - half, 0)
    row = lax.broadcasted_iota(I32, (half, half), 0)

    def part(place, rows):
        value = at_rows(ref, start + place, half)[...].astype(F32)
        return jnp.where(row < rows, value, 0.0)

    first = part(0, kept).astype(BF16)
    second = part(half, over).T.astype(BF16)
    third = part(half + over, over).astype(BF16)
    fourth = part(half + 2 * over, over).astype(BF16)
    top = jnp.concatenate([first, second], axis=1)
    low = jnp.concatenate([third, fourth], axis=1)
    return jnp.concatenate([top, low], axis=0)


class Layout:
    def __init__(self, ways, count, hops):
        self.ways, self.count, self.hops = ways, count, hops
        self.plan = 0
        self.rank = 1
        self.send = self.rank + count
        self.shift = self.send + (ways - 1) * count
        self.start = self.shift + hops * count
        self.source_rank = self.start + hops * count
        self.size = self.source_rank + hops * count


def plan_kernel(lay, half, plans, me_ref, source_ref, *refs):
    ways, count, hops = lay.ways, lay.count, lay.hops
    rank_refs, (table_ref, need_ref, place_ref, all_ref) = refs[:ways], refs[ways:]
    me = me_ref[0]
    for at in range(ways * count * ways):
        need_ref[at] = 0
    for shift in range(ways):
        owner = came_from(me, shift, ways)
        for at in range(count):
            all_ref[owner * count + at] = rank_refs[shift][at]
    for hop in range(hops):
        for taker in range(ways):
            for at in range(count):
                need_ref[source_ref[hop, taker * count + at] * ways + taker] = 1
    largest = [jnp.int32(0)] * ways
    for owner in range(ways):
        for taker in range(ways):
            if owner == taker:
                continue
            shift = next(s for s in range(ways) if partner(owner, s, ways) == taker)
            used = jnp.int32(ROWS)
            for at in range(count):
                source = owner * count + at
                needed = need_ref[source * ways + taker] == 1
                rows = packed_rows(all_ref[source], half)

                @pl.when(owner == me)
                def _():
                    table_ref[lay.send + (shift - 1) * count + at] = jnp.where(needed, used, FAR)

                @pl.when(taker == me)
                def _():
                    place_ref[source] = used

                used = used + jnp.where(needed, rows, 0)
            largest[shift] = jnp.maximum(largest[shift], used)
    chosen = jnp.int32(len(plans) - 1)
    for index in reversed(range(len(plans) - 1)):
        fits = largest[1] <= plans[index][0]
        for shift in range(2, ways):
            fits = fits & (largest[shift] <= plans[index][shift - 1])
        chosen = jnp.where(fits, index, chosen)
    table_ref[lay.plan] = len(plans) - 1 - chosen
    for at in range(count):
        table_ref[lay.rank + at] = rank_refs[0][at]
        for hop in range(hops):
            source = source_ref[hop, me * count + at]
            owner = lax.div(source, count)
            here = owner == me
            slot = hop * count + at
            table_ref[lay.shift + slot] = me ^ owner if ways & (ways - 1) == 0 else (me + (ways - owner)) % ways
            table_ref[lay.start + slot] = jnp.where(here, (source - owner * count) * (4 * half), place_ref[source])
            table_ref[lay.source_rank + slot] = all_ref[source]


def fill_send(lay, half, caps, table_ref, at, shift, own, send_bufs):
    start = jnp.minimum(table_ref[lay.send + (shift - 1) * lay.count + at], caps[shift - 1])
    at_rows(send_bufs[shift - 1], start, 4 * half)[...] = at_rows(own, at * 4 * half, 4 * half)[...]


def send_copies(send_bufs, send_outs, sems):
    return [
        pltpu.make_async_copy(buf.at[pl.ds(0, out.shape[0]), :], out, sems.at[at])
        for at, (buf, out) in enumerate(zip(send_bufs, send_outs))
    ]


def prepare_kernel(half, rank_ref, psi_in, state_ref, image_ref, own_ref, psi, sems):
    def arrival(at):
        return pltpu.make_async_copy(psi_in.at[at], psi.at[at], sems.at[at])

    count = psi.shape[0]
    for at in range(count):
        arrival(at).start()

    @pl.loop(0, count)
    def _(at):
        arrival(at).wait()
        rank = rank_ref[at]
        value = jnp.where(mask_of(rank, 2 * half), psi[at], 0.0)
        state_ref[at] = value
        image_ref[at] = value
        put_packed(own_ref, at * 4 * half, rank, quarters(value))


def send_kernel(lay, half, caps, table_ref, own_ref, sums_ref, *refs):
    sums_ref[...] = jnp.zeros_like(sums_ref)
    number = lay.ways - 1
    send_outs, send_bufs, sems = refs[:number], refs[number : 2 * number], refs[2 * number]
    copies = send_copies(send_bufs, send_outs, sems)
    for shift, copy in enumerate(copies, 1):
        send_bufs[shift - 1][0:ROWS] = jnp.zeros((ROWS, half), BF16)

        @pl.loop(0, lay.count)
        def _(at):
            fill_send(lay, half, caps, table_ref, at, shift, own_ref, send_bufs)

        copy.start()
    for copy in copies:
        copy.wait()


def site_kernel(lay, half, table_ref, own_ref, left_ref, right_ref, out_ref):
    block = get_packed(own_ref, 0, table_ref[lay.rank + pl.program_id(0)], half)
    part = dot(left_ref[0, 0], block).astype(BF16)
    total = dot(part, right_ref[0, 0])

    @pl.when(pl.program_id(1) == 0)
    def _():
        out_ref[0] = total

    @pl.when(pl.program_id(1) != 0)
    def _():
        out_ref[0] += total


def hop_kernel(lay, half, caps, table_ref, turn_ref, step_ref, sums_ref, *refs):
    ways, count, hops = lay.ways, lay.count, lay.hops
    size = 2 * half
    refs = list(refs)

    def take(number):
        out = refs[:number]
        del refs[:number]
        return out

    own_in, *packed_in = take(ways)
    left, right, site, state, image = take(5)
    state_out, image_out, sums_out = take(3)
    own_out, *send_outs = take(ways)
    pool, room, sems = take(3)
    send_bufs = take(ways - 1)

    places = [0, own_in.shape[0]]
    for cap in caps:
        places.append(places[-1] + cap)
    arrivals = [
        pltpu.make_async_copy(ref, pool.at[pl.ds(place, ref.shape[0]), :], sems.at[at])
        for at, (ref, place) in enumerate(zip([own_in, *packed_in], places))
    ]

    for copy in arrivals:
        copy.start()
    for copy in arrivals:
        copy.wait()

    sums = sums_ref[0:3]
    for place in places[1:ways]:
        sums = sums + rows_of_head(pool[place : place + ROWS], room)
    first = turn_ref[0] == 0
    keep, turn = weights(sums, step_ref[0, jnp.maximum(turn_ref[0] - 1, 0)])
    keep_state = jnp.where(first, 1.0, keep)
    keep_image = jnp.where(first, 0.0, keep)
    turn_state = jnp.where(first, 0.0, turn)
    turn_image = jnp.where(first, 1.0, turn)

    def sector(at, sums):
        total = site[at]
        for hop in range(hops):
            slot = hop * count + at
            shift = table_ref[lay.shift + slot]
            start = table_ref[lay.start + slot]
            for way in range(1, ways):
                start = start + jnp.where(shift == way, places[way], 0)
            block = get_packed(pool, start, table_ref[lay.source_rank + slot], half)
            part = dot(left[hop, at], block).astype(BF16)
            total = total + dot(part, right[hop, at])
        rank = table_ref[lay.rank + at]
        before = image[at]
        now = keep_state * state[at] + turn_state * before
        value = keep_image * before + turn_image * jnp.where(mask_of(rank, size), total, 0.0)
        state_out[at] = now
        image_out[at] = value
        put_packed(own_out, at * 4 * half, rank, quarters(value))
        for shift in range(1, ways):
            fill_send(lay, half, caps, table_ref, at, shift, own_out, send_bufs)
        return tuple(
            whole + lane_sums(part) for whole, part in zip(sums, (now * now, now * value, value * value))
        )

    rows = lax.fori_loop(0, count, sector, (jnp.zeros((1, LANES), F32),) * 3, unroll=2)
    sums_out[...] = jnp.zeros_like(sums_out)
    for place, row in enumerate(rows):
        sums_out[place : place + 1] = row

    @pl.when(turn_ref[0] < step_ref.shape[1] - 1)
    def _():
        head = head_of(rows, room)
        for buf in send_bufs:
            buf[0:ROWS] = head
        leaving = send_copies(send_bufs, send_outs, sems)
        for copy in leaving:
            copy.start()
        for copy in leaving:
            copy.wait()


def last_kernel(step, step_ref, state_ref, image_ref, *refs):
    *sums_refs, block_out, weight_out = refs
    keep, turn = weights(sum(ref[0:3] for ref in sums_refs), step_ref[0, step])
    weight_out[0:1] = jnp.broadcast_to(keep, (1, LANES))
    weight_out[1:2] = jnp.broadcast_to(turn, (1, LANES))
    for at in range(state_ref.shape[0]):
        block_out[at] = (keep * state_ref[at] + turn * image_ref[at]).astype(BF16)


def state_kernel(weight_ref, state_ref, image_ref, *refs):
    number = (len(refs) - 2) // 2
    ins, state_out, outs, sems = refs[:number], refs[number], refs[number + 1 : -1], refs[-1]
    copies = [pltpu.make_async_copy(ref, out, sems.at[at]) for at, (ref, out) in enumerate(zip(ins, outs))]
    for copy in copies:
        copy.start()
    keep, turn = weight_ref[0:1, 0:1], weight_ref[1:2, 0:1]
    for at in range(state_ref.shape[0]):
        state_out[at] = keep * state_ref[at] + turn * image_ref[at]
    for copy in copies:
        copy.wait()


def merge_kernel(scale, from_left, from_right, left_next, right_next, left_own, right_own, left_out, right_out, left_buf, right_buf, sems):
    terms, count = left_next.shape[:2]

    def leaving(term, at):
        return (
            pltpu.make_async_copy(left_buf.at[term, at], left_out.at[term, at], sems.at[0, term, at]),
            pltpu.make_async_copy(right_buf.at[term, at], right_out.at[term, at], sems.at[1, term, at]),
        )

    def sector(at, done):
        a = from_left[at]
        b = from_right[at]
        a_turned = a.astype(F32).T.astype(BF16)
        b_turned = b.astype(F32).T.astype(BF16)
        lefts = [dot(a_turned, left_next[term, at]).astype(BF16) for term in range(terms)]
        rights = [dot(right_next[term, at], b_turned).astype(BF16) for term in range(terms)]
        for term in range(terms):
            left_copy, right_copy = leaving(term, at)
            left_buf[term, at] = left_own[term, at].astype(F32) + scale * dot(lefts[term], a)
            left_copy.start()
            right_buf[term, at] = right_own[term, at].astype(F32) + scale * dot(b, rights[term])
            right_copy.start()
        return done

    lax.fori_loop(0, count, sector, 0, unroll=2)
    for term in range(terms):
        for at in range(count):
            for copy in leaving(term, at):
                copy.wait()


def run_kernel(body, args, in_specs, out_shape, out_specs, *, flops=0, grid=(), scratch=(), reuse=None, room=VMEM_BYTES):
    moved = sum(a.size * a.dtype.itemsize for a in args)
    moved += sum(math.prod(s.shape) * jnp.dtype(s.dtype).itemsize for s in out_shape)
    return pl.pallas_call(
        body,
        grid=grid,
        in_specs=in_specs,
        out_specs=out_specs,
        out_shape=out_shape,
        scratch_shapes=list(scratch),
        input_output_aliases=reuse or {},
        compiler_params=pltpu.CompilerParams(vmem_limit_bytes=room),
        cost_estimate=pl.CostEstimate(flops=flops, bytes_accessed=moved, transcendentals=0),
    )(*args)


def on_device(psi, kept_rank, step_size, left_env, right_env, hop_left, hop_right, hop_source):
    count, size = psi.shape[1], psi.shape[2]
    half = size // 2
    terms, hops = left_env.shape[1], hop_left.shape[1]
    ways = lax.axis_size("sector")
    chi_total = count * ways * size
    lay = Layout(ways, count, hops)
    left_one, right_one = left_env[0], right_env[0]
    hop_first, hop_second = hop_left[0], hop_right[0]
    full = count * 4 * half
    plans = [tuple(ROWS * (full * part // (64 * ROWS)) + ROWS for part in plan) for plan in PLANS if len(plan) == ways - 1]
    if not plans:
        plans = [(full + ROWS,) * (ways - 1)]

    smem = pl.BlockSpec(memory_space=pltpu.SMEM)
    vmem = pl.BlockSpec(memory_space=pltpu.VMEM)
    anywhere = pl.BlockSpec(memory_space=pl.ANY)
    square = pl.BlockSpec((1, size, size), lambda t, term: (t, 0, 0))
    packed = pl.BlockSpec((4 * half, half), lambda t, term: (t, 0))
    single = pl.BlockSpec((1, 1, size, size), lambda t, term: (term, t, 0, 0))
    block_f32 = jax.ShapeDtypeStruct((count, size, size), F32)
    here_f32 = pltpu.VMEM((count, size, size), F32)
    block_b16 = jax.ShapeDtypeStruct((count, size, size), BF16)
    here_own = pltpu.VMEM((full, half), BF16)
    sums_shape = jax.ShapeDtypeStruct((8, LANES), F32)
    flop = 2 * size**3

    rank = kept_rank[0]
    ranks = [rank] + [exchange(rank, "sector", shift) for shift in range(1, ways)]
    left_next = from_behind(left_one, "chain", 1)
    right_next = from_behind(right_one, "chain", -1)
    state, image, own = run_kernel(
        functools.partial(prepare_kernel, half),
        (rank, psi[0]),
        [smem, pl.BlockSpec(memory_space=pltpu.HBM)],
        [here_f32, here_f32, here_own],
        [vmem] * 3,
        scratch=[pltpu.VMEM((count, size, size), F32), pltpu.SemaphoreType.DMA((count,))],
        room=MOST_BYTES,
    )
    me = lax.axis_index("sector").astype(I32).reshape(1)
    (table,) = run_kernel(
        functools.partial(plan_kernel, lay, half, plans),
        (me, hop_source, *ranks),
        [smem] * (2 + ways),
        [jax.ShapeDtypeStruct((lay.size,), I32)],
        [smem],
        room=MOST_BYTES,
        scratch=[
            pltpu.SMEM((ways * count * ways,), I32),
            pltpu.SMEM((ways * count,), I32),
            pltpu.SMEM((ways * count,), I32),
        ],
    )

    def update(caps, state, image, own, table, step_size, left_one, right_one, hop_first, hop_second):
        send_shapes = [jax.ShapeDtypeStruct((cap, half), BF16) for cap in caps]
        bufs = [pltpu.VMEM((cap + 4 * half, half), BF16) for cap in caps]
        sums, *sends = run_kernel(
            functools.partial(send_kernel, lay, half, caps),
            (table, own),
            [smem, vmem],
            [sums_shape, *send_shapes],
            [vmem] + [anywhere] * (ways - 1),
            scratch=bufs + [pltpu.SemaphoreType.DMA((ways - 1,))],
        )

        def step(turn, carried):
            state, image, sums, own, *sends = carried
            arrived = [exchange(send, "sector", 1 + at) for at, send in enumerate(sends)]
            (site,) = run_kernel(
                functools.partial(site_kernel, lay, half),
                (table, own, left_one, right_one),
                [smem, packed, single, single],
                [block_f32],
                [square],
                flops=count * terms * 2 * flop,
                grid=(count, terms),
            )
            outs = run_kernel(
                functools.partial(hop_kernel, lay, half, caps),
                (table, turn.reshape(1), step_size, sums, own, *arrived, hop_first, hop_second, site, state, image),
                [smem, smem, smem, vmem] + [anywhere] * ways + [vmem] * 5,
                [here_f32, here_f32, sums_shape, here_own, *send_shapes],
                [vmem] * 4 + [anywhere] * (ways - 1),
                flops=count * hops * 2 * flop,
                scratch=[
                    pltpu.VMEM((full + sum(caps) + 4 * half, half), BF16),
                    pltpu.VMEM((ROWS, half), F32),
                    pltpu.SemaphoreType.DMA((ways,)),
                    *bufs,
                ],
                reuse={4: 3, 7 + ways: 0, 8 + ways: 1},
            )
            return list(outs)

        state, image, sums, *_ = lax.fori_loop(0, step_size.shape[1], step, [state, image, sums, own, *sends])
        return state, image, sums

    state, image, sums = lax.switch(
        table[lay.plan],
        [functools.partial(update, caps) for caps in reversed(plans)],
        state, image, own, table, step_size, left_one, right_one, hop_first, hop_second,
    )
    every = [sums] + [exchange(sums, "sector", shift) for shift in range(1, ways)]
    block, weight = run_kernel(
        functools.partial(last_kernel, step_size.shape[1] - 1),
        (step_size, state, image, *every),
        [smem] + [vmem] * (2 + ways),
        [block_b16, pltpu.VMEM((8, LANES), F32)],
        [vmem, vmem],
    )
    from_left = from_behind(block, "chain", 1)
    from_right = from_behind(block, "chain", -1)
    envs = (left_next, right_next, left_one, right_one)
    state, *envs = run_kernel(
        state_kernel,
        (weight, state, image, *envs),
        [vmem] * 3 + [anywhere] * len(envs),
        [block_f32] + [pltpu.VMEM(env.shape, BF16) for env in envs],
        [vmem] * (1 + len(envs)),
        scratch=[pltpu.SemaphoreType.DMA((len(envs),))],
    )
    env_f32 = jax.ShapeDtypeStruct((terms, count, size, size), F32)
    merged_left, merged_right = run_kernel(
        functools.partial(merge_kernel, float(chi_total)),
        (from_left, from_right, *envs),
        [vmem] * 6,
        [env_f32, env_f32],
        [anywhere, anywhere],
        flops=count * terms * 4 * flop,
        scratch=[
            pltpu.VMEM((terms, count, size, size), F32),
            pltpu.VMEM((terms, count, size, size), F32),
            pltpu.SemaphoreType.DMA((2, terms, count)),
        ],
    )
    return (state[None], merged_left[None], merged_right[None])


def solution(mesh):
    placed = (
        P("chain", "sector", None, None),
        P("chain", "sector"),
        P("chain", None),
        P("chain", None, "sector", None, None),
        P("chain", None, "sector", None, None),
        P("chain", None, "sector", None, None),
        P("chain", None, "sector", None, None),
        P(),
    )
    return jax.shard_map(
        on_device,
        mesh=mesh,
        in_specs=placed,
        out_specs=(
            P("chain", "sector", None, None),
            P("chain", None, "sector", None, None),
            P("chain", None, "sector", None, None),
        ),
        check_vma=False,
    )
```

```python
import functools
import math

import jax
import jax.numpy as jnp
from jax import lax
from jax.experimental import pallas as pl
from jax.experimental.pallas import tpu as pltpu
from jax.sharding import PartitionSpec as P

LANES = 128
ROWS = 16
FAR = 1 << 20
F32 = jnp.float32
BF16 = jnp.bfloat16
I32 = jnp.int32
VMEM_BYTES = 20 * 1024 * 1024
MOST_BYTES = 56 * 1024 * 1024
PLANS = (
    (48, 28, 22),
    (52, 20, 34),
    (44, 38, 22),
    (48, 28, 32),
    (60, 32, 28),
    (56, 26, 38),
    (52, 34, 34),
    (60, 22, 46),
    (48, 44, 28),
    (44, 38, 38),
    (52, 32, 48),
    (60, 48, 32),
    (60, 44, 44),
    (36, 34, 56),
    (44, 56, 34),
    (36, 50, 50),
    (64, 64, 64),
)


def from_behind(value, axis, steps):
    count = lax.axis_size(axis)
    initial, last = (max(0, -steps), min(count, count - steps))
    return lax.ppermute(value, axis, [(source, source + steps) for source in range(initial, last)])


def partner(index, shift, ways):
    return index ^ shift if ways & (ways - 1) == 0 else (index + shift) % ways


def came_from(index, shift, ways):
    return index ^ shift if ways & (ways - 1) == 0 else (index + (ways - shift)) % ways


def exchange(value, axis, shift):
    count = lax.axis_size(axis)
    return lax.ppermute(value, axis, [(source, partner(source, shift, count)) for source in range(count)])


def dot(a, b):
    return jnp.dot(a, b, preferred_element_type=F32)


def mask_of(rank, size):
    rows = lax.broadcasted_iota(I32, (size, size), 0)
    cols = lax.broadcasted_iota(I32, (size, size), 1)
    return (rows < rank) & (cols < rank)


def weights(sums, step_now):
    total = jnp.sum(sums, axis=1, keepdims=True)
    self_dot, cross, image_dot = total[0:1], total[1:2], total[2:3]
    quotient = cross / self_dot
    state_resid = cross - quotient * self_dot
    resid_dot = image_dot - 2.0 * quotient * cross + quotient * quotient * self_dot
    new_dot = self_dot - 2.0 * step_now * state_resid + step_now * step_now * resid_dot
    norm = jnp.sqrt(new_dot)
    return (1.0 + step_now * quotient) / norm, -step_now / norm


def lane_sums(value):
    rows = jnp.sum(value, axis=0, keepdims=True)
    total = rows[:, 0:LANES]
    for at in range(LANES, rows.shape[1], LANES):
        total = total + rows[:, at : at + LANES]
    return total


def head_of(rows, room_ref):
    room_ref[...] = jnp.zeros_like(room_ref)
    for place, row in enumerate(rows):
        for part in range(3):
            now = row.astype(BF16).astype(F32)
            room_ref[3 * part + place : 3 * part + place + 1] = now
            row = row - now
    return room_ref[...].astype(BF16)


def rows_of_head(head, room_ref):
    room_ref[...] = head.astype(F32)
    return room_ref[0:3] + room_ref[3:6] + room_ref[6:9]


def kept_rows(rank):
    return (rank + (ROWS - 1)) & ~(ROWS - 1)


def packed_rows(rank, half):
    rows = kept_rows(rank)
    return jnp.where(rows <= half, rows, 3 * rows - 2 * half)


def at_rows(ref, start, rows):
    return ref.at[pl.ds(pl.multiple_of(start, ROWS), rows), :]


def quarters(value):
    half = value.shape[0] // 2
    return (
        value[:half, :half].astype(BF16),
        value[:half, half:].T.astype(BF16),
        value[half:, :half].astype(BF16),
        value[half:, half:].astype(BF16),
    )


def put_packed(ref, start, rank, parts):
    half = parts[0].shape[0]
    over = jnp.maximum(kept_rows(rank) - half, 0)
    for place, part in zip((0, half, half + over, half + 2 * over), parts):
        at_rows(ref, start + place, half)[...] = part


def get_packed(ref, start, rank, half):
    kept = kept_rows(rank)
    over = jnp.maximum(kept - half, 0)
    row = lax.broadcasted_iota(I32, (half, half), 0)

    def part(place, rows):
        value = at_rows(ref, start + place, half)[...].astype(F32)
        return jnp.where(row < rows, value, 0.0)

    first = part(0, kept).astype(BF16)
    second = part(half, over).T.astype(BF16)
    third = part(half + over, over).astype(BF16)
    fourth = part(half + 2 * over, over).astype(BF16)
    top = jnp.concatenate([first, second], axis=1)
    low = jnp.concatenate([third, fourth], axis=1)
    return jnp.concatenate([top, low], axis=0)


class Layout:
    def __init__(self, ways, count, hops):
        self.ways, self.count, self.hops = ways, count, hops
        self.plan = 0
        self.rank = 1
        self.send = self.rank + count
        self.shift = self.send + (ways - 1) * count
        self.start = self.shift + hops * count
        self.source_rank = self.start + hops * count
        self.size = self.source_rank + hops * count


def plan_kernel(lay, half, plans, me_ref, source_ref, *refs):
    ways, count, hops = lay.ways, lay.count, lay.hops
    rank_refs, (table_ref, need_ref, place_ref, all_ref) = refs[:ways], refs[ways:]
    me = me_ref[0]
    for at in range(ways * count * ways):
        need_ref[at] = 0
    for shift in range(ways):
        owner = came_from(me, shift, ways)
        for at in range(count):
            all_ref[owner * count + at] = rank_refs[shift][at]
    for hop in range(hops):
        for taker in range(ways):
            for at in range(count):
                need_ref[source_ref[hop, taker * count + at] * ways + taker] = 1
    largest = [jnp.int32(0)] * ways
    for owner in range(ways):
        for taker in range(ways):
            if owner == taker:
                continue
            shift = next(s for s in range(ways) if partner(owner, s, ways) == taker)
            used = jnp.int32(ROWS)
            for at in range(count):
                source = owner * count + at
                needed = need_ref[source * ways + taker] == 1
                rows = packed_rows(all_ref[source], half)

                @pl.when(owner == me)
                def _():
                    table_ref[lay.send + (shift - 1) * count + at] = jnp.where(needed, used, FAR)

                @pl.when(taker == me)
                def _():
                    place_ref[source] = used

                used = used + jnp.where(needed, rows, 0)
            largest[shift] = jnp.maximum(largest[shift], used)
    chosen = jnp.int32(len(plans) - 1)
    for index in reversed(range(len(plans) - 1)):
        fits = largest[1] <= plans[index][0]
        for shift in range(2, ways):
            fits = fits & (largest[shift] <= plans[index][shift - 1])
        chosen = jnp.where(fits, index, chosen)
    table_ref[lay.plan] = len(plans) - 1 - chosen
    for at in range(count):
        table_ref[lay.rank + at] = rank_refs[0][at]
        for hop in range(hops):
            source = source_ref[hop, me * count + at]
            owner = lax.div(source, count)
            here = owner == me
            slot = hop * count + at
            table_ref[lay.shift + slot] = me ^ owner if ways & (ways - 1) == 0 else (me + (ways - owner)) % ways
            table_ref[lay.start + slot] = jnp.where(here, (source - owner * count) * (4 * half), place_ref[source])
            table_ref[lay.source_rank + slot] = all_ref[source]


def fill_send(lay, half, caps, table_ref, at, shift, own, send_bufs):
    start = jnp.minimum(table_ref[lay.send + (shift - 1) * lay.count + at], caps[shift - 1])
    at_rows(send_bufs[shift - 1], start, 4 * half)[...] = at_rows(own, at * 4 * half, 4 * half)[...]


def send_copies(send_bufs, send_outs, sems):
    return [
        pltpu.make_async_copy(buf.at[pl.ds(0, out.shape[0]), :], out, sems.at[at])
        for at, (buf, out) in enumerate(zip(send_bufs, send_outs))
    ]


def prepare_kernel(half, rank_ref, psi_in, state_ref, image_ref, own_ref, psi, sems):
    def arrival(at):
        return pltpu.make_async_copy(psi_in.at[at], psi.at[at], sems.at[at])

    count = psi.shape[0]
    for at in range(count):
        arrival(at).start()

    @pl.loop(0, count)
    def _(at):
        arrival(at).wait()
        rank = rank_ref[at]
        value = jnp.where(mask_of(rank, 2 * half), psi[at], 0.0)
        state_ref[at] = value
        image_ref[at] = value
        put_packed(own_ref, at * 4 * half, rank, quarters(value))


def send_kernel(lay, half, caps, table_ref, own_ref, sums_ref, *refs):
    sums_ref[...] = jnp.zeros_like(sums_ref)
    number = lay.ways - 1
    send_outs, send_bufs, sems = refs[:number], refs[number : 2 * number], refs[2 * number]
    copies = send_copies(send_bufs, send_outs, sems)
    for shift, copy in enumerate(copies, 1):
        send_bufs[shift - 1][0:ROWS] = jnp.zeros((ROWS, half), BF16)

        @pl.loop(0, lay.count)
        def _(at):
            fill_send(lay, half, caps, table_ref, at, shift, own_ref, send_bufs)

        copy.start()
    for copy in copies:
        copy.wait()


def site_kernel(lay, half, table_ref, own_ref, left_ref, right_ref, out_ref):
    block = get_packed(own_ref, 0, table_ref[lay.rank + pl.program_id(0)], half)
    part = dot(left_ref[0, 0], block).astype(BF16)
    total = dot(part, right_ref[0, 0])

    @pl.when(pl.program_id(1) == 0)
    def _():
        out_ref[0] = total

    @pl.when(pl.program_id(1) != 0)
    def _():
        out_ref[0] += total


def hop_kernel(lay, half, caps, table_ref, turn_ref, step_ref, sums_ref, *refs):
    ways, count, hops = lay.ways, lay.count, lay.hops
    size = 2 * half
    refs = list(refs)

    def take(number):
        out = refs[:number]
        del refs[:number]
        return out

    own_in, *packed_in = take(ways)
    left, right, site, state, image = take(5)
    state_out, image_out, sums_out = take(3)
    own_out, *send_outs = take(ways)
    pool, room, sems = take(3)
    send_bufs = take(ways - 1)

    places = [0, own_in.shape[0]]
    for cap in caps:
        places.append(places[-1] + cap)
    arrivals = [
        pltpu.make_async_copy(ref, pool.at[pl.ds(place, ref.shape[0]), :], sems.at[at])
        for at, (ref, place) in enumerate(zip([own_in, *packed_in], places))
    ]

    for copy in arrivals:
        copy.start()
    for copy in arrivals:
        copy.wait()

    sums = sums_ref[0:3]
    for place in places[1:ways]:
        sums = sums + rows_of_head(pool[place : place + ROWS], room)
    first = turn_ref[0] == 0
    more = turn_ref[0] < step_ref.shape[1] - 1
    keep, turn = weights(sums, step_ref[0, jnp.maximum(turn_ref[0] - 1, 0)])
    keep_state = jnp.where(first, 1.0, keep)
    keep_image = jnp.where(first, 0.0, keep)
    turn_state = jnp.where(first, 0.0, turn)
    turn_image = jnp.where(first, 1.0, turn)

    def sector(at, sums):
        total = site[at]
        for hop in range(hops):
            slot = hop * count + at
            shift = table_ref[lay.shift + slot]
            start = table_ref[lay.start + slot]
            for way in range(1, ways):
                start = start + jnp.where(shift == way, places[way], 0)
            block = get_packed(pool, start, table_ref[lay.source_rank + slot], half)
            part = dot(left[hop, at], block).astype(BF16)
            total = total + dot(part, right[hop, at])
        rank = table_ref[lay.rank + at]
        before = image[at]
        now = keep_state * state[at] + turn_state * before
        value = keep_image * before + turn_image * jnp.where(mask_of(rank, size), total, 0.0)
        state_out[at] = now
        image_out[at] = value

        @pl.when(more)
        def _():
            put_packed(own_out, at * 4 * half, rank, quarters(value))
            for shift in range(1, ways):
                fill_send(lay, half, caps, table_ref, at, shift, own_out, send_bufs)

        return tuple(
            whole + lane_sums(part) for whole, part in zip(sums, (now * now, now * value, value * value))
        )

    rows = lax.fori_loop(0, count, sector, (jnp.zeros((1, LANES), F32),) * 3, unroll=2)
    sums_out[...] = jnp.zeros_like(sums_out)
    for place, row in enumerate(rows):
        sums_out[place : place + 1] = row

    @pl.when(more)
    def _():
        head = head_of(rows, room)
        for buf in send_bufs:
            buf[0:ROWS] = head
        leaving = send_copies(send_bufs, send_outs, sems)
        for copy in leaving:
            copy.start()
        for copy in leaving:
            copy.wait()


def last_kernel(step, step_ref, state_ref, image_ref, *refs):
    *sums_refs, block_out, weight_out = refs
    keep, turn = weights(sum(ref[0:3] for ref in sums_refs), step_ref[0, step])
    weight_out[0:1] = jnp.broadcast_to(keep, (1, LANES))
    weight_out[1:2] = jnp.broadcast_to(turn, (1, LANES))
    for at in range(state_ref.shape[0]):
        block_out[at] = (keep * state_ref[at] + turn * image_ref[at]).astype(BF16)


def state_kernel(weight_ref, state_ref, image_ref, *refs):
    number = (len(refs) - 2) // 2
    ins, state_out, outs, sems = refs[:number], refs[number], refs[number + 1 : -1], refs[-1]
    copies = [pltpu.make_async_copy(ref, out, sems.at[at]) for at, (ref, out) in enumerate(zip(ins, outs))]
    for copy in copies:
        copy.start()
    keep, turn = weight_ref[0:1, 0:1], weight_ref[1:2, 0:1]
    for at in range(state_ref.shape[0]):
        state_out[at] = keep * state_ref[at] + turn * image_ref[at]
    for copy in copies:
        copy.wait()


def merge_kernel(scale, from_left, from_right, left_next, right_next, left_own, right_own, left_out, right_out, left_buf, right_buf, sems):
    terms, count = left_next.shape[:2]

    def leaving(term, at):
        return (
            pltpu.make_async_copy(left_buf.at[term, at], left_out.at[term, at], sems.at[0, term, at]),
            pltpu.make_async_copy(right_buf.at[term, at], right_out.at[term, at], sems.at[1, term, at]),
        )

    def sector(at, done):
        a = from_left[at]
        b = from_right[at]
        a_turned = a.astype(F32).T.astype(BF16)
        b_turned = b.astype(F32).T.astype(BF16)
        lefts = [dot(a_turned, left_next[term, at]).astype(BF16) for term in range(terms)]
        rights = [dot(right_next[term, at], b_turned).astype(BF16) for term in range(terms)]
        for term in range(terms):
            left_copy, right_copy = leaving(term, at)
            left_buf[term, at] = left_own[term, at].astype(F32) + scale * dot(lefts[term], a)
            left_copy.start()
            right_buf[term, at] = right_own[term, at].astype(F32) + scale * dot(b, rights[term])
            right_copy.start()
        return done

    lax.fori_loop(0, count, sector, 0, unroll=2)
    for term in range(terms):
        for at in range(count):
            for copy in leaving(term, at):
                copy.wait()


def run_kernel(body, args, in_specs, out_shape, out_specs, *, flops=0, grid=(), scratch=(), reuse=None, room=VMEM_BYTES):
    moved = sum(a.size * a.dtype.itemsize for a in args)
    moved += sum(math.prod(s.shape) * jnp.dtype(s.dtype).itemsize for s in out_shape)
    return pl.pallas_call(
        body,
        grid=grid,
        in_specs=in_specs,
        out_specs=out_specs,
        out_shape=out_shape,
        scratch_shapes=list(scratch),
        input_output_aliases=reuse or {},
        compiler_params=pltpu.CompilerParams(vmem_limit_bytes=room),
        cost_estimate=pl.CostEstimate(flops=flops, bytes_accessed=moved, transcendentals=0),
    )(*args)


def on_device(psi, kept_rank, step_size, left_env, right_env, hop_left, hop_right, hop_source):
    count, size = psi.shape[1], psi.shape[2]
    half = size // 2
    terms, hops = left_env.shape[1], hop_left.shape[1]
    ways = lax.axis_size("sector")
    chi_total = count * ways * size
    lay = Layout(ways, count, hops)
    left_one, right_one = left_env[0], right_env[0]
    hop_first, hop_second = hop_left[0], hop_right[0]
    full = count * 4 * half
    plans = [tuple(ROWS * (full * part // (64 * ROWS)) + ROWS for part in plan) for plan in PLANS if len(plan) == ways - 1]
    if not plans:
        plans = [(full + ROWS,) * (ways - 1)]

    smem = pl.BlockSpec(memory_space=pltpu.SMEM)
    vmem = pl.BlockSpec(memory_space=pltpu.VMEM)
    anywhere = pl.BlockSpec(memory_space=pl.ANY)
    square = pl.BlockSpec((1, size, size), lambda t, term: (t, 0, 0))
    packed = pl.BlockSpec((4 * half, half), lambda t, term: (t, 0))
    single = pl.BlockSpec((1, 1, size, size), lambda t, term: (term, t, 0, 0))
    block_f32 = jax.ShapeDtypeStruct((count, size, size), F32)
    here_f32 = pltpu.VMEM((count, size, size), F32)
    block_b16 = jax.ShapeDtypeStruct((count, size, size), BF16)
    here_own = pltpu.VMEM((full, half), BF16)
    sums_shape = jax.ShapeDtypeStruct((8, LANES), F32)
    flop = 2 * size**3

    rank = kept_rank[0]
    ranks = [rank] + [exchange(rank, "sector", shift) for shift in range(1, ways)]
    left_next = from_behind(left_one, "chain", 1)
    right_next = from_behind(right_one, "chain", -1)
    state, image, own = run_kernel(
        functools.partial(prepare_kernel, half),
        (rank, psi[0]),
        [smem, pl.BlockSpec(memory_space=pltpu.HBM)],
        [here_f32, here_f32, here_own],
        [vmem] * 3,
        scratch=[pltpu.VMEM((count, size, size), F32), pltpu.SemaphoreType.DMA((count,))],
        room=MOST_BYTES,
    )
    me = lax.axis_index("sector").astype(I32).reshape(1)
    (table,) = run_kernel(
        functools.partial(plan_kernel, lay, half, plans),
        (me, hop_source, *ranks),
        [smem] * (2 + ways),
        [jax.ShapeDtypeStruct((lay.size,), I32)],
        [smem],
        room=MOST_BYTES,
        scratch=[
            pltpu.SMEM((ways * count * ways,), I32),
            pltpu.SMEM((ways * count,), I32),
            pltpu.SMEM((ways * count,), I32),
        ],
    )

    def update(caps, state, image, own, table, step_size, left_one, right_one, hop_first, hop_second):
        send_shapes = [jax.ShapeDtypeStruct((cap, half), BF16) for cap in caps]
        bufs = [pltpu.VMEM((cap + 4 * half, half), BF16) for cap in caps]
        sums, *sends = run_kernel(
            functools.partial(send_kernel, lay, half, caps),
            (table, own),
            [smem, vmem],
            [sums_shape, *send_shapes],
            [vmem] + [anywhere] * (ways - 1),
            scratch=bufs + [pltpu.SemaphoreType.DMA((ways - 1,))],
        )

        def step(turn, carried):
            state, image, sums, own, *sends = carried
            arrived = [exchange(send, "sector", 1 + at) for at, send in enumerate(sends)]
            (site,) = run_kernel(
                functools.partial(site_kernel, lay, half),
                (table, own, left_one, right_one),
                [smem, packed, single, single],
                [block_f32],
                [square],
                flops=count * terms * 2 * flop,
                grid=(count, terms),
            )
            outs = run_kernel(
                functools.partial(hop_kernel, lay, half, caps),
                (table, turn.reshape(1), step_size, sums, own, *arrived, hop_first, hop_second, site, state, image),
                [smem, smem, smem, vmem] + [anywhere] * ways + [vmem] * 5,
                [here_f32, here_f32, sums_shape, here_own, *send_shapes],
                [vmem] * 4 + [anywhere] * (ways - 1),
                flops=count * hops * 2 * flop,
                scratch=[
                    pltpu.VMEM((full + sum(caps) + 4 * half, half), BF16),
                    pltpu.VMEM((ROWS, half), F32),
                    pltpu.SemaphoreType.DMA((ways,)),
                    *bufs,
                ],
                reuse={4: 3, 7 + ways: 0, 8 + ways: 1},
            )
            return list(outs)

        state, image, sums, *_ = lax.fori_loop(0, step_size.shape[1], step, [state, image, sums, own, *sends])
        return state, image, sums

    state, image, sums = lax.switch(
        table[lay.plan],
        [functools.partial(update, caps) for caps in reversed(plans)],
        state, image, own, table, step_size, left_one, right_one, hop_first, hop_second,
    )
    every = [sums] + [exchange(sums, "sector", shift) for shift in range(1, ways)]
    block, weight = run_kernel(
        functools.partial(last_kernel, step_size.shape[1] - 1),
        (step_size, state, image, *every),
        [smem] + [vmem] * (2 + ways),
        [block_b16, pltpu.VMEM((8, LANES), F32)],
        [vmem, vmem],
    )
    from_left = from_behind(block, "chain", 1)
    from_right = from_behind(block, "chain", -1)
    envs = (left_next, right_next, left_one, right_one)
    state, *envs = run_kernel(
        state_kernel,
        (weight, state, image, *envs),
        [vmem] * 3 + [anywhere] * len(envs),
        [block_f32] + [pltpu.VMEM(env.shape, BF16) for env in envs],
        [vmem] * (1 + len(envs)),
        scratch=[pltpu.SemaphoreType.DMA((len(envs),))],
    )
    env_f32 = jax.ShapeDtypeStruct((terms, count, size, size), F32)
    merged_left, merged_right = run_kernel(
        functools.partial(merge_kernel, float(chi_total)),
        (from_left, from_right, *envs),
        [vmem] * 6,
        [env_f32, env_f32],
        [anywhere, anywhere],
        flops=count * terms * 4 * flop,
        scratch=[
            pltpu.VMEM((terms, count, size, size), F32),
            pltpu.VMEM((terms, count, size, size), F32),
            pltpu.SemaphoreType.DMA((2, terms, count)),
        ],
    )
    return (state[None], merged_left[None], merged_right[None])


def solution(mesh):
    placed = (
        P("chain", "sector", None, None),
        P("chain", "sector"),
        P("chain", None),
        P("chain", None, "sector", None, None),
        P("chain", None, "sector", None, None),
        P("chain", None, "sector", None, None),
        P("chain", None, "sector", None, None),
        P(),
    )
    return jax.shard_map(
        on_device,
        mesh=mesh,
        in_specs=placed,
        out_specs=(
            P("chain", "sector", None, None),
            P("chain", None, "sector", None, None),
            P("chain", None, "sector", None, None),
        ),
        check_vma=False,
    )
```
